256 devices in a mesh: section: 16 (over y_hi, x, core), tensor: 16 (over y_lo, z).
Axes of the slice: x: 4, y: 4 (y_hi: 2, y_lo: 2; y = y_hi * 2 + y_lo), z: 8, core: 2. Of those that a mesh axis runs over, the one named last changes fastest.
Arguments:
- x_saved: bfloat16 [16, 2, 256, 4608], P('section', None, None, 'tensor'), may hold values from -12 to 12
- grad_first: bfloat16 [16, 256, 4608], P('section', None, 'tensor'), may hold values from -6 to 6
- gains: float32 [32, 4608], replicated, may hold values from 0.1 to 1.9
- assign: int32 [16, 2], P('section'), may hold values from 0 to 31
- order: int32 [16], replicated, may hold values from 0 to 1
- w_query: bfloat16 [4608, 4096], P(None, 'tensor'), may hold values from -0.088388348 to 0.088388348
- w_key: bfloat16 [4608, 2048], P(None, 'tensor'), may hold values from -0.088388348 to 0.088388348
- w_value: bfloat16 [4608, 2048], P(None, 'tensor'), may hold values from -0.09375 to 0.09375
- w_output: bfloat16 [4096, 4608], P('tensor'), may hold values from -0.09375 to 0.09375
Outputs:
- input_grad: bfloat16 [16, 256, 4608], P('section', None, 'tensor')
- grad_query: float32 [4608, 4096], P('section', 'tensor')
- grad_key: float32 [4608, 2048], P('section', 'tensor')
- grad_value: float32 [4608, 2048], P('section', 'tensor')
- grad_output: float32 [4096, 4608], P('tensor', 'section')
The draws below stay inside these ranges and needn't reach their ends.
All inputs are finite; a program needn't handle non-finite values.
Results may differ from the reference program's by a relative error of at most 0.033.
Values may be sent and summed in bfloat16 or wider, within the bound.
No kernel may reach another device: no remote copies, remote signals or barrier semaphores. Data moves between devices by JAX's collectives and lax.ppermute only.
A program may use at most 128 MiB of HBM per device.

```python
import jax
import jax.numpy as jnp
from jax import lax

D = 4608
HEADS = 32
KV = 16
HD = 128
TOK = 256
ITERS = 32
N_SECTION = 16


def query_base(key):
    values = jax.random.normal(key, (D, HEADS * HD), jnp.float32)
    return jnp.clip(values, -6.0, 6.0) * D ** (-0.5)


def draw_w_query(key, part):
    shared = query_base(key)
    return shared.astype(jnp.bfloat16)


def draw_w_key(key, part):
    key = jax.random.fold_in(key, 22)
    values = jax.random.normal(key, (D, KV * HD), jnp.float32)
    return (jnp.clip(values, -6.0, 6.0) * D ** (-0.5)).astype(jnp.bfloat16)


def draw_x_saved(key, part):
    key = jax.random.fold_in(key, 11)
    key_base = jax.random.fold_in(key, 0)
    key_perm = jax.random.fold_in(key, 2)
    shape = (N_SECTION, 2, TOK, D)
    block = D // N_SECTION
    perm = jax.random.permutation(key_perm, N_SECTION)
    owner = lax.broadcasted_iota(jnp.int32, (N_SECTION, D), 1) // block
    spike = jnp.where(owner == perm[:, None], 3.0, 1.0).astype(jnp.float32)[:, None, None, :]
    base = jnp.clip(jax.random.normal(key_base, shape, jnp.float32), -4.0, 4.0) * spike
    return jnp.clip(base, -12.0, 12.0).astype(jnp.bfloat16)


def touch_ends(drawn, key, least, high):
    extent = drawn.shape
    index_at = [jax.random.randint(jax.random.fold_in(key, axis), (), 0, extent[axis]) for axis in range(len(extent))]
    drawn = drawn.at[tuple(index_at)].set(least)
    longest = extent.index(max(extent))
    index_at[longest] = (index_at[longest] + 1) % extent[longest]
    return drawn.at[tuple(index_at)].set(high)


def shard_levels(rng, dims, cuts, least, largest):
    factor_of = 1.0
    for axis_at, shards_of in cuts:
        heights = jax.random.uniform(jax.random.fold_in(jax.random.fold_in(rng, 6), axis_at), (shards_of,), jnp.float32, least / len(cuts), largest / len(cuts))
        factor_of = factor_of * jnp.repeat(jnp.exp(heights), dims[axis_at] // shards_of).reshape((-1,) + (1,) * (len(dims) - 1 - axis_at))
    return factor_of


def scatter_about(own_key, shape, scale, most, pieces=(), held_as=jnp.bfloat16):
    drawn = scale * jax.random.normal(own_key, shape, jnp.float32)
    if pieces:
        drawn = drawn * shard_levels(own_key, shape, pieces, -0.22, 0.18)
    return jnp.clip(drawn, -most, most).astype(held_as)


def setup_inputs(seed: int = 0) -> dict:
    seeds = jax.random.split(jax.random.key(seed), 10)
    return {
        "x_saved": draw_x_saved(jax.random.fold_in(seeds[9], 71), 0),
        "grad_first": scatter_about(seeds[1], (N_SECTION, TOK, D), 1.0, 6.0, ((0, 16), (2, 16))),
        "gains": jnp.clip(1.0 + 0.18 * jax.random.normal(seeds[2], (ITERS, D), jnp.float32), 0.1, 1.9),
        "assign": touch_ends(jax.random.randint(seeds[3], (N_SECTION, 2), 0, ITERS), jax.random.fold_in(seeds[3], 1), 0, ITERS - 1).astype(jnp.int32),
        "order": touch_ends(jax.random.randint(seeds[4], (N_SECTION,), 0, 2), jax.random.fold_in(seeds[4], 1), 0, 1).astype(jnp.int32),
        "w_query": draw_w_query(jax.random.fold_in(seeds[9], 71), 0),
        "w_key": draw_w_key(jax.random.fold_in(seeds[9], 71), 0),
        "w_value": scatter_about(seeds[7], (D, KV * HD), D ** -0.5, 0.09375, ((1, 16),)),
        "w_output": scatter_about(seeds[8], (HEADS * HD, D), (HEADS * HD) ** -0.5, 0.09375, ((0, 16),)),
    }


def attention_pass(inputs, scale_row, upstream, w_query, w_key, w_value, w_output):
    f32 = jnp.float32
    tokens = inputs.shape[0]
    group = HEADS // KV
    factor = HD ** -0.5
    scaled = (inputs.astype(f32) * scale_row).astype(jnp.bfloat16)
    query = jnp.dot(scaled, w_query, preferred_element_type=f32).astype(jnp.bfloat16).reshape(tokens, HEADS, HD)
    keys = jnp.dot(scaled, w_key, preferred_element_type=f32).astype(jnp.bfloat16).reshape(tokens, KV, HD)
    values = jnp.dot(scaled, w_value, preferred_element_type=f32).astype(jnp.bfloat16).reshape(tokens, KV, HD)
    keys_rep = jnp.repeat(keys, group, axis=1)
    values_rep = jnp.repeat(values, group, axis=1)
    scores = jnp.einsum("thd,uhd->htu", query.astype(f32), keys_rep.astype(f32)) * factor
    rows = lax.broadcasted_iota(jnp.int32, (tokens, tokens), 0)
    cols = lax.broadcasted_iota(jnp.int32, (tokens, tokens), 1)
    causal = (cols <= rows)[None]
    scores = jnp.where(causal, scores, -1e30)
    top = jnp.max(scores, axis=-1, keepdims=True)
    expo = jnp.where(causal, jnp.exp(scores - top), 0.0)
    probs = expo / jnp.sum(expo, axis=-1, keepdims=True)
    probs_b = probs.astype(jnp.bfloat16)
    attended = jnp.einsum("htu,uhd->thd", probs_b.astype(f32), values_rep.astype(f32)).astype(jnp.bfloat16)
    attended = attended.reshape(tokens, HEADS * HD)
    grad_att = jnp.einsum("td,cd->tc", upstream.astype(f32), w_output.astype(f32)).astype(jnp.bfloat16)
    grad_heads = grad_att.reshape(tokens, HEADS, HD)
    grad_probs = jnp.einsum("thd,uhd->htu", grad_heads.astype(f32), values_rep.astype(f32))
    delta = jnp.sum(probs * grad_probs, axis=-1, keepdims=True)
    grad_scores = (probs * (grad_probs - delta) * factor).astype(jnp.bfloat16)
    grad_query = jnp.einsum("htu,uhd->thd", grad_scores.astype(f32), keys_rep.astype(f32)).astype(jnp.bfloat16)
    grad_key_full = jnp.einsum("htu,thd->uhd", grad_scores.astype(f32), query.astype(f32))
    grad_key = grad_key_full.reshape(tokens, KV, group, HD).sum(axis=2).astype(jnp.bfloat16)
    grad_val_full = jnp.einsum("htu,thd->uhd", probs_b.astype(f32), grad_heads.astype(f32))
    grad_value = grad_val_full.reshape(tokens, KV, group, HD).sum(axis=2).astype(jnp.bfloat16)
    grad_query = grad_query.reshape(tokens, HEADS * HD)
    grad_key = grad_key.reshape(tokens, KV * HD)
    grad_value = grad_value.reshape(tokens, KV * HD)
    branch = (jnp.einsum("tc,dc->td", grad_query.astype(f32), w_query.astype(f32))
              + jnp.einsum("tc,dc->td", grad_key.astype(f32), w_key.astype(f32))
              + jnp.einsum("tc,dc->td", grad_value.astype(f32), w_value.astype(f32)))
    result = (upstream.astype(f32) + scale_row * branch).astype(jnp.bfloat16)
    part_query = jnp.einsum("td,tc->dc", scaled.astype(f32), grad_query.astype(f32))
    part_key = jnp.einsum("td,tc->dc", scaled.astype(f32), grad_key.astype(f32))
    part_value = jnp.einsum("td,tc->dc", scaled.astype(f32), grad_value.astype(f32))
    part_output = jnp.einsum("tc,td->cd", attended.astype(f32), upstream.astype(f32))
    return result, (part_query, part_key, part_value, part_output)


def reference(x_saved, grad_first, gains, assign, order, w_query, w_key, w_value, w_output):
    weights = (w_query, w_key, w_value, w_output)

    def run_pass(section, which, upstream):
        if which == 0:
            batch = order[section]
        else:
            batch = order[(section + 1) % N_SECTION]
        inputs = x_saved[section, batch]
        scale_row = gains[assign[section, which]]
        return attention_pass(inputs, scale_row, upstream, *weights)

    start_grad, unused = run_pass(0, 0, grad_first[0])

    def visit(carry, section):
        upstream, totals = carry
        first_dx, first_parts = run_pass(section, 0, grad_first[section])
        second_dx, second_parts = run_pass(section, 1, upstream)
        rounded = tuple((a + b).astype(jnp.bfloat16).astype(jnp.float32) for a, b in zip(first_parts, second_parts))
        totals = tuple(t + r for t, r in zip(totals, rounded))
        return (first_dx, totals), second_dx

    zeros = (jnp.zeros((D, HEADS * HD), jnp.float32), jnp.zeros((D, KV * HD), jnp.float32),
             jnp.zeros((D, KV * HD), jnp.float32), jnp.zeros((HEADS * HD, D), jnp.float32))
    sections = jnp.arange(N_SECTION - 1, -1, -1, dtype=jnp.int32)
    (unused_grad, totals), outputs = lax.scan(visit, (start_grad, zeros), sections)
    input_grad = outputs[::-1]
    return input_grad, totals[0], totals[1], totals[2], totals[3]
```

```python
import functools

import jax
import jax.numpy as jnp
from jax import lax
from jax.experimental import pallas as pl
from jax.experimental.pallas import tpu as pltpu
from jax.sharding import PartitionSpec as P

HD = 128
F32 = jnp.float32
BF16 = jnp.bfloat16
ROW = (((1,), (0,)), ((), ()))
NT = (((1,), (1,)), ((), ()))
TN = (((0,), (0,)), ((), ()))


def mul(a, b, dims):
    return lax.dot_general(a, b, dims, preferred_element_type=F32)


def along_z(by):
    return [(t, (t & 8) | ((t + by) & 7)) for t in range(16)]


def along_x(by):
    return [(s, (s & 9) | ((((s >> 1) + by) & 3) << 1)) for s in range(16)]


SWAP_Y = [(t, t ^ 8) for t in range(16)]
SWAP_CORE = [(s, s ^ 1) for s in range(16)]
SWAP_YHI = [(s, s ^ 8) for s in range(16)]


def to_previous(flip):
    pairs = []
    for s in range(16):
        for t in range(16):
            pairs.append((s * 16 + t, ((s - 1) % 16) * 16 + (t ^ flip)))
    return pairs


def send(a, axis, pairs):
    return lax.ppermute(a, axis, pairs)


def ring(payload):
    up, down = payload, payload
    found = {0: payload}
    for step in (1, 2, 3):
        up = send(up, "tensor", along_z(1))
        down = send(down, "tensor", along_z(-1))
        found[-step] = up
        found[step] = down
    far = (
        send(up[:, :144], "tensor", along_z(1)),
        send(down[:, 144:], "tensor", along_z(-1)),
    )
    return found, far


def assemble_kernel(routes, inputs, place_ref, *refs):
    ins, outs, sems = refs[:inputs], refs[inputs:-1], refs[-1]
    copies = []
    for number, (source, row, target, plane, offset, half) in enumerate(routes):
        depth = (place_ref[1] + offset) % 8
        if plane is None:
            dst = outs[target].at[depth]
        else:
            level = (place_ref[0] + plane) % 2 if plane < 2 else plane - 2
            dst = outs[target].at[level, depth]
        if half is not None:
            dst = dst.at[pl.ds(half * 144, 144)]
        copy = pltpu.make_async_copy(ins[source].at[row], dst, sems.at[number])
        copy.start()
        copies.append(copy)
    for copy in copies:
        copy.wait()


def assemble(arrays, routes, out_shapes, place):
    any_space = pl.BlockSpec(memory_space=pl.ANY)
    return pl.pallas_call(
        functools.partial(assemble_kernel, routes, len(arrays)),
        out_shape=[jax.ShapeDtypeStruct(shape, BF16) for shape in out_shapes],
        in_specs=[pl.BlockSpec(memory_space=pltpu.SMEM)] + [any_space] * len(arrays),
        out_specs=[any_space] * len(out_shapes),
        scratch_shapes=[pltpu.SemaphoreType.DMA((len(routes),))],
        cost_estimate=pl.CostEstimate(flops=0, bytes_accessed=5000000, transcendentals=0),
    )(place, *arrays)


class Routes:
    def __init__(self):
        self.arrays, self.routes = [], []

    def add(self, array, pieces):
        at = len(self.arrays)
        self.arrays.append(array)
        for row, (target, plane, offset, half) in enumerate(pieces):
            self.routes.append((at, row, target, plane, offset, half))


def scatter_chain(parts, plane, z):
    def part(offset):
        place = (z + offset) % 8
        return lax.dynamic_slice(parts, (plane, place, 0, 0), (1, 1, 288, 256))[0, 0]

    far = part(4)
    up = send(far[:144], "tensor", along_z(1))
    down = send(far[144:], "tensor", along_z(-1))
    near = part(3)
    up = jnp.concatenate([near[:144] + up, near[144:]], axis=0)
    near = part(-3)
    down = jnp.concatenate([near[:144], near[144:] + down], axis=0)
    for step in (2, 1, 0):
        up = send(up, "tensor", along_z(1))
        down = send(down, "tensor", along_z(-1))
        if step:
            up = part(step) + up
            down = part(-step) + down
    return part(0).astype(F32) + up.astype(F32) + down.astype(F32)


def section_scatter(mine, core, x, yhi):
    columns = mine.shape[-1]

    def side(which):
        return lax.dynamic_slice(mine, (0, 0, which, 0, 0), (2, 4, 1, 288, columns))[:, :, 0]

    both = side(core) + send(side(1 - core), "section", SWAP_CORE)

    def part(offset):
        return lax.dynamic_slice(both, (0, (x + offset) % 4, 0, 0), (2, 1, 288, columns))[:, 0]

    far = part(2)
    up = send(far[:1], "section", along_x(1))
    down = send(far[1:], "section", along_x(-1))
    near = part(1)
    up = jnp.concatenate([near[:1] + up, near[1:]], axis=0)
    near = part(-1)
    down = jnp.concatenate([near[:1], near[1:] + down], axis=0)
    up = send(up, "section", along_x(1))
    down = send(down, "section", along_x(-1))
    total = part(0).astype(F32) + up.astype(F32) + down.astype(F32)
    away = lax.dynamic_slice(total, (1 - yhi, 0, 0), (1, 288, columns))[0].astype(BF16)
    keep = lax.dynamic_slice(total, (yhi, 0, 0), (1, 288, columns))[0]
    return keep + send(away, "section", SWAP_YHI).astype(F32)


def forward(n, weights):
    proj = mul(weights, n, TN).astype(BF16)
    q, k, v = proj[:256], proj[256:384], proj[384:]
    j = lax.broadcasted_iota(jnp.int32, (256, 256), 0)
    i = lax.broadcasted_iota(jnp.int32, (256, 256), 1)
    causal = j <= i
    probs, outs = [], []
    for h in range(2):
        scores = mul(k, q[h * HD : (h + 1) * HD], TN) * (HD**-0.5)
        scores = jnp.where(causal, scores, -1e30)
        top = jnp.max(scores, axis=0, keepdims=True)
        expo = jnp.where(causal, jnp.exp(scores - top), 0.0)
        p = expo / jnp.sum(expo, axis=0, keepdims=True)
        probs.append(p)
        outs.append(mul(v, p.astype(BF16), ROW).astype(BF16))
    return q, k, v, probs, jnp.concatenate(outs, axis=0)


def backward(saved, g, w_output):
    q, k, v, probs, _ = saved
    d_o = mul(w_output, g, ROW).astype(BF16)
    d_q, d_k, d_v = [], 0.0, 0.0
    for h in range(2):
        d_oh = d_o[h * HD : (h + 1) * HD]
        p = probs[h]
        dp = mul(v, d_oh, TN)
        delta = jnp.sum(p * dp, axis=0, keepdims=True)
        ds = (p * (dp - delta) * (HD**-0.5)).astype(BF16)
        d_q.append(mul(k, ds, ROW).astype(BF16))
        d_k = d_k + mul(q[h * HD : (h + 1) * HD], ds, NT)
        d_v = d_v + mul(d_oh, p.astype(BF16), NT)
    return jnp.concatenate(d_q + [d_k.astype(BF16), d_v.astype(BF16)], axis=0)


def body(x_saved, grad_first, gains, assign, order, w_query, w_key, w_value, w_output):
    s = lax.axis_index("section")
    t = lax.axis_index("tensor")
    z, y = t % 8, t // 8
    core, x, yhi = s % 2, (s // 2) % 4, s // 8
    place = jnp.stack([y, z]).astype(jnp.int32)
    shares = gains.reshape(32, 16, 288)
    previous = [(i, (i - 1) % 16) for i in range(16)]

    def share(which, shard):
        return lax.dynamic_slice(shares, (which, shard, 0), (1, 1, 288)).reshape(288, 1)

    first_share = share(assign[0, 0], t)
    second_share = share(assign[0, 1], t)
    own_batch = lax.dynamic_slice(order, (s,), (1,))[0]
    next_batch = lax.dynamic_slice(order, ((s + 1) % 16,), (1,))[0]

    def scaled(batch, scale):
        rows = jnp.where(batch == 0, x_saved[0, 0], x_saved[0, 1])
        return (rows.T.astype(F32) * scale).astype(BF16)

    full = (2, 8, 288, 256)
    plane = (8, 288, 256)

    own = jnp.stack([scaled(own_batch, first_share), grad_first[0].T])
    other = send(own, "tensor", SWAP_Y)
    found, far = ring(own)
    found_n, far_n = ring(other[:1])
    routes = Routes()
    for offset, block in found.items():
        routes.add(block, [(0, 0, offset, None), (1, 0, offset, None)])
    for half in (0, 1):
        routes.add(far[half], [(0, 0, 4, half), (1, 0, 4, half)])
    for offset, block in found_n.items():
        if offset:
            routes.add(block, [(0, 1, offset, None)])
    for half in (0, 1):
        routes.add(far_n[half], [(0, 1, 4, half)])
    routes.add(other, [(0, 1, 0, None), (1, 1, 0, None)])
    for step in (1, 2, 3):
        swapped = send(jnp.stack([found[step][1], found[-step][1]]), "tensor", SWAP_Y)
        routes.add(swapped, [(1, 1, step, None), (1, 1, -step, None)])
    swapped = send(jnp.stack([far[0][1], far[1][1]]), "tensor", SWAP_Y)
    routes.add(swapped, [(1, 1, 4, 0), (1, 1, 4, 1)])
    n1_full, g1_full = assemble(routes.arrays, routes.routes, [full, full], place)
    n1_full = n1_full.reshape(4608, 256)
    g1_full = g1_full.reshape(4608, 256)

    g1_next = send(own[1], "section", previous), send(other[1], "section", previous)
    g1_next = jnp.where(y == 0, g1_next[0], g1_next[1]), jnp.where(y == 0, g1_next[1], g1_next[0])
    which_next = send(assign, "section", previous)[0, 0]

    n2, unused = lax.optimization_barrier((scaled(next_batch, second_share), far_n[0]))
    found, far = ring(n2[None])
    routes = Routes()
    for offset, block in found.items():
        routes.add(block, [(0, None, offset, None)])
    for half in (0, 1):
        routes.add(far[half], [(0, None, 4, half)])
    (n2_plane,) = assemble(routes.arrays, routes.routes, [plane], place)
    n2_other = send(n2_plane, "tensor", SWAP_Y)
    n2_full = jnp.where(
        y == 0, jnp.stack([n2_plane, n2_other]), jnp.stack([n2_other, n2_plane])
    ).reshape(4608, 256)

    weights = jnp.concatenate([w_query, w_key, w_value], axis=1)
    saved1 = forward(n1_full, weights)
    proj1 = backward(saved1, g1_full, w_output)
    dn1 = mul(weights, proj1, ROW).astype(BF16).reshape(full)
    g2 = []
    routes = Routes()
    for chain in (0, 1):
        part1 = scatter_chain(dn1, chain, z).astype(BF16)
        here = send(part1, ("section", "tensor"), to_previous(0))
        there = send(part1, ("section", "tensor"), to_previous(8))
        branch = here.astype(F32) + there.astype(F32)
        scale = share(which_next, z + 8 * chain)
        shard = (g1_next[chain].astype(F32) + scale * branch).astype(BF16)
        g2.append(shard)
        found, far = ring(shard[None])
        for offset, block in found.items():
            routes.add(block, [(0, 2 + chain, offset, None)])
        for half in (0, 1):
            routes.add(far[half], [(0, 2 + chain, 4, half)])
    (g2_full,) = assemble(routes.arrays, routes.routes, [full], place)
    g2_full = g2_full.reshape(4608, 256)

    grads1 = jnp.concatenate([mul(n1_full, proj1, NT), mul(g1_full, saved1[4], NT)], axis=1)
    grads1 = lax.psum_scatter(grads1.astype(BF16), "section", scatter_dimension=0, tiled=True)

    saved2 = forward(n2_full, weights)
    proj2 = backward(saved2, g2_full, w_output)
    right2 = mul(g2_full, saved2[4], NT).astype(BF16).reshape(2, 4, 2, 288, 256)
    right2 = section_scatter(right2, core, x, yhi)

    dn2 = mul(weights, proj2, ROW).astype(BF16).reshape(full)
    part2 = [scatter_chain(dn2, chain, z) for chain in (0, 1)]
    away = jnp.where(y == 0, part2[1], part2[0]).astype(BF16)
    keep = jnp.where(y == 0, part2[0], part2[1])
    dn2_own = keep + send(away, "tensor", SWAP_Y).astype(F32)
    g2_own = jnp.where(y == 0, g2[0], g2[1])
    dx2 = (g2_own.astype(F32) + second_share * dn2_own).astype(BF16)

    left2 = mul(n2_full, proj2, NT).astype(BF16).reshape(2, 4, 2, 288, 512)
    left2 = section_scatter(left2, core, x, yhi)
    left = grads1[:, :512].astype(F32) + left2
    right = grads1[:, 512:].astype(F32) + right2
    return (
        dx2.T[None],
        left[:, :256],
        left[:, 256:384],
        left[:, 384:],
        right.T,
    )


def solution(mesh):
    in_specs = (
        P("section", None, None, "tensor"),
        P("section", None, "tensor"),
        P(),
        P("section", None),
        P(),
        P(None, "tensor"),
        P(None, "tensor"),
        P(None, "tensor"),
        P("tensor", None),
    )
    out_specs = (
        P("section", None, "tensor"),
        P("section", "tensor"),
        P("section", "tensor"),
        P("section", "tensor"),
        P("tensor", "section"),
    )
    return jax.shard_map(body, mesh=mesh, in_specs=in_specs, out_specs=out_specs, check_vma=False)
```

```python
import functools

import jax
import jax.numpy as jnp
from jax import lax
from jax.experimental import pallas as pl
from jax.experimental.pallas import tpu as pltpu
from jax.sharding import PartitionSpec as P

HD = 128
F32 = jnp.float32
BF16 = jnp.bfloat16
ROW = (((1,), (0,)), ((), ()))
NT = (((1,), (1,)), ((), ()))
TN = (((0,), (0,)), ((), ()))


def mul(a, b, dims):
    return lax.dot_general(a, b, dims, preferred_element_type=F32)


def along_z(by):
    return [(t, (t & 8) | ((t + by) & 7)) for t in range(16)]


def along_x(by):
    return [(s, (s & 9) | ((((s >> 1) + by) & 3) << 1)) for s in range(16)]


SWAP_Y = [(t, t ^ 8) for t in range(16)]
SWAP_CORE = [(s, s ^ 1) for s in range(16)]
SWAP_YHI = [(s, s ^ 8) for s in range(16)]


def to_previous(flip):
    pairs = []
    for s in range(16):
        for t in range(16):
            pairs.append((s * 16 + t, ((s - 1) % 16) * 16 + (t ^ flip)))
    return pairs


def send(a, axis, pairs):
    return lax.ppermute(a, axis, pairs)


def ring(payload):
    up, down = payload, payload
    found = {0: payload}
    for step in (1, 2, 3):
        up = send(up, "tensor", along_z(1))
        down = send(down, "tensor", along_z(-1))
        found[-step] = up
        found[step] = down
    far = (
        send(up[:, :144], "tensor", along_z(1)),
        send(down[:, 144:], "tensor", along_z(-1)),
    )
    return found, far


def assemble_kernel(routes, inputs, place_ref, *refs):
    ins, outs, sems = refs[:inputs], refs[inputs:-1], refs[-1]
    copies = []
    for number, (source, row, target, plane, offset, half) in enumerate(routes):
        depth = (place_ref[1] + offset) % 8
        if plane is None:
            dst = outs[target].at[depth]
        else:
            level = (place_ref[0] + plane) % 2 if plane < 2 else plane - 2
            dst = outs[target].at[level, depth]
        if half is not None:
            dst = dst.at[pl.ds(half * 144, 144)]
        copy = pltpu.make_async_copy(ins[source].at[row], dst, sems.at[number])
        copy.start()
        copies.append(copy)
    for copy in copies:
        copy.wait()


ANY = pl.BlockSpec(memory_space=pl.ANY)
SMEM = pl.BlockSpec(memory_space=pltpu.SMEM)
VMEM = pl.BlockSpec(memory_space=pltpu.VMEM)


def params(mib):
    return pltpu.CompilerParams(vmem_limit_bytes=mib * 2**20)


def cost(flops, moved):
    return pl.CostEstimate(flops=flops, bytes_accessed=moved, transcendentals=0)


def assemble(arrays, routes, out_shapes, place):
    return pl.pallas_call(
        functools.partial(assemble_kernel, routes, len(arrays)),
        out_shape=[jax.ShapeDtypeStruct(shape, BF16) for shape in out_shapes],
        in_specs=[SMEM] + [ANY] * len(arrays),
        out_specs=[VMEM] * len(out_shapes),
        scratch_shapes=[pltpu.SemaphoreType.DMA((len(routes),))],
        compiler_params=params(24),
        cost_estimate=cost(0, 10000000),
    )(place, *arrays)


def both_products_kernel(n_ref, proj_ref, g_ref, o_ref, out_ref):
    out_ref[:, :512] = mul(n_ref[...], proj_ref[...], NT).astype(BF16)
    out_ref[:, 512:] = mul(g_ref[...], o_ref[...], NT).astype(BF16)


def both_products(n, proj, g, o):
    rows = 1152
    tall = pl.BlockSpec((rows, 256), lambda i: (i, 0))
    return pl.pallas_call(
        both_products_kernel,
        grid=(4608 // rows,),
        out_shape=jax.ShapeDtypeStruct((4608, 768), BF16),
        in_specs=[
            tall,
            pl.BlockSpec((512, 256), lambda i: (0, 0)),
            tall,
            pl.BlockSpec((256, 256), lambda i: (0, 0)),
        ],
        out_specs=pl.BlockSpec((rows, 768), lambda i: (i, 0)),
        compiler_params=params(32),
        cost_estimate=cost(2 * 4608 * 768 * 256, 12000000),
    )(n, proj, g, o)


def sided_product_kernel(flip, place_ref, n_ref, proj_ref, out_ref):
    core, x, yhi = place_ref[2], place_ref[3], place_ref[4]
    side = core if flip == 0 else 1 - core
    for ahead in range(4):
        for over in range(2):
            level = yhi if over == 0 else 1 - yhi
            slot = (level * 4 + (x + ahead) % 4) * 2 + side
            out_ref[ahead, over] = mul(n_ref[slot], proj_ref[...], NT).astype(BF16)


def sided_product(flip, place, n, proj):
    columns = proj.shape[0]
    return pl.pallas_call(
        functools.partial(sided_product_kernel, flip),
        out_shape=jax.ShapeDtypeStruct((4, 2, 288, columns), BF16),
        in_specs=[SMEM, VMEM, VMEM],
        out_specs=VMEM,
        compiler_params=params(24),
        cost_estimate=cost(2304 * 256 * 2 * columns, 5000000),
    )(place, n.reshape(16, 288, 256), proj)


def branch_kernel(place_ref, w_ref, proj_ref, out_ref):
    for ahead in range(8):
        depth = (place_ref[1] + ahead) % 8
        for plane in range(2):
            out_ref[ahead, plane] = mul(w_ref[plane, depth], proj_ref[...], ROW).astype(BF16)


def branch(place, weights, proj):
    return pl.pallas_call(
        branch_kernel,
        out_shape=jax.ShapeDtypeStruct((8, 2, 288, 256), BF16),
        in_specs=[SMEM, VMEM, VMEM],
        out_specs=VMEM,
        compiler_params=params(24),
        cost_estimate=cost(2 * 4608 * 512 * 256, 7000000),
    )(place, weights.reshape(2, 8, 288, 512), proj)


class Routes:
    def __init__(self):
        self.arrays, self.routes = [], []

    def add(self, array, pieces):
        at = len(self.arrays)
        self.arrays.append(array)
        for row, (target, plane, offset, half) in enumerate(pieces):
            self.routes.append((at, row, target, plane, offset, half))


def scatter_start(far):
    up = send(far[:, :144], "tensor", along_z(1))
    down = send(far[:, 144:], "tensor", along_z(-1))
    return up, down


def scatter_rest(parts, up, down):
    up = jnp.concatenate([parts[3][:, :144] + up, parts[3][:, 144:]], axis=1)
    down = jnp.concatenate([parts[5][:, :144], parts[5][:, 144:] + down], axis=1)
    for step in (2, 1, 0):
        up = send(up, "tensor", along_z(1))
        down = send(down, "tensor", along_z(-1))
        if step:
            up = parts[step] + up
            down = parts[8 - step] + down
    return parts[0].astype(F32) + up.astype(F32) + down.astype(F32)


def section_scatter(keep, away):
    came = send(away, "section", SWAP_CORE)
    up = send(keep[2, 0] + came[2, 0], "section", along_x(1))
    down = send(keep[2, 1] + came[2, 1], "section", along_x(-1))
    near = keep[1] + came[1]
    up = jnp.stack([near[0] + up, near[1]])
    near = keep[3] + came[3]
    down = jnp.stack([near[0], near[1] + down])
    up = send(up, "section", along_x(1))
    down = send(down, "section", along_x(-1))
    total = keep[0].astype(F32) + came[0].astype(F32) + up.astype(F32) + down.astype(F32)
    return total[0] + send(total[1].astype(BF16), "section", SWAP_YHI).astype(F32)


def forward(n, weights):
    proj = mul(weights, n, TN).astype(BF16)
    q, k, v = proj[:256], proj[256:384], proj[384:]
    j = lax.broadcasted_iota(jnp.int32, (256, 256), 0)
    i = lax.broadcasted_iota(jnp.int32, (256, 256), 1)
    causal = j <= i
    probs, outs = [], []
    for h in range(2):
        scores = mul(k, q[h * HD : (h + 1) * HD], TN) * (HD**-0.5)
        scores = jnp.where(causal, scores, -1e30)
        top = jnp.max(scores, axis=0, keepdims=True)
        expo = jnp.where(causal, jnp.exp(scores - top), 0.0)
        p = expo / jnp.sum(expo, axis=0, keepdims=True)
        probs.append(p)
        outs.append(mul(v, p.astype(BF16), ROW).astype(BF16))
    return q, k, v, probs, jnp.concatenate(outs, axis=0)


def backward(saved, g, w_output):
    q, k, v, probs, _ = saved
    d_o = mul(w_output, g, ROW).astype(BF16)
    d_q, d_k, d_v = [], 0.0, 0.0
    for h in range(2):
        d_oh = d_o[h * HD : (h + 1) * HD]
        p = probs[h]
        dp = mul(v, d_oh, TN)
        delta = jnp.sum(p * dp, axis=0, keepdims=True)
        ds = (p * (dp - delta) * (HD**-0.5)).astype(BF16)
        d_q.append(mul(k, ds, ROW).astype(BF16))
        d_k = d_k + mul(q[h * HD : (h + 1) * HD], ds, NT)
        d_v = d_v + mul(d_oh, p.astype(BF16), NT)
    return jnp.concatenate(d_q + [d_k.astype(BF16), d_v.astype(BF16)], axis=0)


def body(x_saved, grad_first, gains, assign, order, w_query, w_key, w_value, w_output):
    s = lax.axis_index("section")
    t = lax.axis_index("tensor")
    z, y = t % 8, t // 8
    place = jnp.stack([y, z, s % 2, (s // 2) % 4, s // 8]).astype(jnp.int32)
    previous = [(i, (i - 1) % 16) for i in range(16)]

    def share(which, shard):
        return lax.dynamic_slice(gains, (which, shard * 288), (1, 288)).reshape(288, 1)

    second_share = share(assign[0, 1], t)
    own_batch = lax.dynamic_slice(order, (s,), (1,))[0]
    next_batch = lax.dynamic_slice(order, ((s + 1) % 16,), (1,))[0]

    def scaled(batch, scale):
        rows = jnp.where(batch == 0, x_saved[0, 0], x_saved[0, 1])
        return (rows.T.astype(F32) * scale).astype(BF16)

    full = (2, 8, 288, 256)
    plane = (8, 288, 256)

    own = jnp.stack(
        [
            scaled(own_batch, share(assign[0, 0], t)),
            grad_first[0].T,
            scaled(next_batch, second_share),
        ]
    )
    other = send(own[:2], "tensor", SWAP_Y)
    found, far = ring(own)
    found_n, far_n = ring(other[:1])
    routes = Routes()
    for offset, block in found.items():
        routes.add(block, [(0, 0, offset, None), (1, 0, offset, None), (2, None, offset, None)])
    for half in (0, 1):
        routes.add(far[half], [(0, 0, 4, half), (1, 0, 4, half), (2, None, 4, half)])
    for offset, block in found_n.items():
        if offset:
            routes.add(block, [(0, 1, offset, None)])
    for half in (0, 1):
        routes.add(far_n[half], [(0, 1, 4, half)])
    routes.add(other, [(0, 1, 0, None), (1, 1, 0, None)])
    for step in (1, 2, 3):
        swapped = send(jnp.stack([found[step][1], found[-step][1]]), "tensor", SWAP_Y)
        routes.add(swapped, [(1, 1, step, None), (1, 1, -step, None)])
    swapped = send(jnp.stack([far[0][1], far[1][1]]), "tensor", SWAP_Y)
    routes.add(swapped, [(1, 1, 4, 0), (1, 1, 4, 1)])
    n1_full, g1_full, n2_plane = assemble(
        routes.arrays, routes.routes, [full, full, plane], place
    )
    n1_full = n1_full.reshape(4608, 256)
    g1_full = g1_full.reshape(4608, 256)

    g1_next = send(own[1], "section", previous), send(other[1], "section", previous)
    g1_next = jnp.where(y == 0, g1_next[0], g1_next[1]), jnp.where(y == 0, g1_next[1], g1_next[0])
    which_next = send(assign, "section", previous)[0, 0]

    weights = jnp.concatenate([w_query, w_key, w_value], axis=1)
    saved1 = forward(n1_full, weights)
    proj1 = backward(saved1, g1_full, w_output)
    dn1 = branch(place, weights, proj1)
    starts = [scatter_start(dn1[4][chain : chain + 1]) for chain in (0, 1)]

    n2_other = send(n2_plane, "tensor", SWAP_Y)
    grads1 = both_products(n1_full, proj1, g1_full, saved1[4])
    dn1, grads1 = lax.optimization_barrier((dn1, grads1))
    grads1 = lax.psum_scatter(grads1, "section", scatter_dimension=0, tiled=True)

    n2_full = jnp.where(
        y == 0, jnp.stack([n2_plane, n2_other]), jnp.stack([n2_other, n2_plane])
    ).reshape(4608, 256)
    saved2 = forward(n2_full, weights)
    g2 = []
    routes = Routes()
    for chain in (0, 1):
        part1 = scatter_rest(dn1[:, chain : chain + 1], *starts[chain])[0].astype(BF16)
        here = send(part1, ("section", "tensor"), to_previous(0))
        there = send(part1, ("section", "tensor"), to_previous(8))
        total = here.astype(F32) + there.astype(F32)
        scale = share(which_next, z + 8 * chain)
        shard = (g1_next[chain].astype(F32) + scale * total).astype(BF16)
        if chain == 1:
            shard, outs = lax.optimization_barrier((shard, saved2[4]))
            saved2 = saved2[:4] + (outs,)
        g2.append(shard)
        found, far = ring(shard[None])
        for offset, block in found.items():
            routes.add(block, [(0, 2 + chain, offset, None)])
        for half in (0, 1):
            routes.add(far[half], [(0, 2 + chain, 4, half)])
    (g2_full,) = assemble(routes.arrays, routes.routes, [full], place)
    g2_full = g2_full.reshape(4608, 256)

    proj2 = backward(saved2, g2_full, w_output)
    right2 = section_scatter(
        sided_product(0, place, g2_full, saved2[4]), sided_product(1, place, g2_full, saved2[4])
    )

    dn2 = branch(place, weights, proj2)
    part2 = scatter_rest(dn2, *scatter_start(dn2[4]))
    away = jnp.where(y == 0, part2[1], part2[0]).astype(BF16)
    keep = jnp.where(y == 0, part2[0], part2[1])
    dn2_own = keep + send(away, "tensor", SWAP_Y).astype(F32)
    g2_own = jnp.where(y == 0, g2[0], g2[1])
    dx2 = (g2_own.astype(F32) + second_share * dn2_own).astype(BF16)

    left2 = section_scatter(
        sided_product(0, place, n2_full, proj2), sided_product(1, place, n2_full, proj2)
    )
    left = grads1[:, :512].astype(F32) + left2
    right = grads1[:, 512:].astype(F32) + right2
    return (
        dx2.T[None],
        left[:, :256],
        left[:, 256:384],
        left[:, 384:],
        right.T,
    )


def solution(mesh):
    in_specs = (
        P("section", None, None, "tensor"),
        P("section", None, "tensor"),
        P(),
        P("section", None),
        P(),
        P(None, "tensor"),
        P(None, "tensor"),
        P(None, "tensor"),
        P("tensor", None),
    )
    out_specs = (
        P("section", None, "tensor"),
        P("section", "tensor"),
        P("section", "tensor"),
        P("section", "tensor"),
        P("tensor", "section"),
    )
    return jax.shard_map(body, mesh=mesh, in_specs=in_specs, out_specs=out_specs, check_vma=False)
```

```python
import functools

import jax
import jax.numpy as jnp
from jax import lax
from jax.experimental import pallas as pl
from jax.experimental.pallas import tpu as pltpu
from jax.sharding import PartitionSpec as P

HD = 128
F32 = jnp.float32
BF16 = jnp.bfloat16
ROW = (((1,), (0,)), ((), ()))
NT = (((1,), (1,)), ((), ()))
TN = (((0,), (0,)), ((), ()))


def mul(a, b, dims):
    return lax.dot_general(a, b, dims, preferred_element_type=F32)


def along_z(by):
    return [(t, (t & 8) | ((t + by) & 7)) for t in range(16)]


def along_x(by):
    return [(s, (s & 9) | ((((s >> 1) + by) & 3) << 1)) for s in range(16)]


SWAP_Y = [(t, t ^ 8) for t in range(16)]
SWAP_CORE = [(s, s ^ 1) for s in range(16)]
SWAP_YHI = [(s, s ^ 8) for s in range(16)]


def to_previous(flip):
    pairs = []
    for s in range(16):
        for t in range(16):
            pairs.append((s * 16 + t, ((s - 1) % 16) * 16 + (t ^ flip)))
    return pairs


def send(a, axis, pairs):
    return lax.ppermute(a, axis, pairs)


def ring(payload):
    up, down = payload, payload
    found = {0: payload}
    for step in (1, 2, 3):
        up = send(up, "tensor", along_z(1))
        down = send(down, "tensor", along_z(-1))
        found[-step] = up
        found[step] = down
    far = (
        send(up[:, :144], "tensor", along_z(1)),
        send(down[:, 144:], "tensor", along_z(-1)),
    )
    return found, far


def place_blocks(routes, place_ref, ins, outs, sems):
    copies = []
    for number, (source, row, target, plane, offset, half) in enumerate(routes):
        depth = (place_ref[1] + offset) % 8
        if plane is None:
            dst = outs[target].at[depth]
        else:
            level = (place_ref[0] + plane) % 2 if plane < 2 else plane - 2
            dst = outs[target].at[level, depth]
        if half is not None:
            dst = dst.at[pl.ds(half * 144, 144)]
        copy = pltpu.make_async_copy(ins[source].at[row], dst, sems.at[number])
        copy.start()
        copies.append(copy)
    return copies


def assemble_kernel(routes, inputs, place_ref, *refs):
    for copy in place_blocks(routes, place_ref, refs[:inputs], refs[inputs:-1], refs[-1]):
        copy.wait()


ANY = pl.BlockSpec(memory_space=pl.ANY)
SMEM = pl.BlockSpec(memory_space=pltpu.SMEM)
VMEM = pl.BlockSpec(memory_space=pltpu.VMEM)


def params(mib):
    return pltpu.CompilerParams(vmem_limit_bytes=mib * 2**20)


def cost(flops, moved):
    return pl.CostEstimate(flops=flops, bytes_accessed=moved, transcendentals=0)


def assemble(arrays, routes, out_shapes, place):
    return pl.pallas_call(
        functools.partial(assemble_kernel, routes, len(arrays)),
        out_shape=[jax.ShapeDtypeStruct(shape, BF16) for shape in out_shapes],
        in_specs=[SMEM] + [ANY] * len(arrays),
        out_specs=[VMEM] * len(out_shapes),
        scratch_shapes=[pltpu.SemaphoreType.DMA((len(routes),))],
        compiler_params=params(56),
        cost_estimate=cost(0, 10000000),
    )(place, *arrays)


def both_products_kernel(n_ref, proj_ref, g_ref, o_ref, out_ref):
    out_ref[:, :512] = mul(n_ref[...], proj_ref[...], NT).astype(BF16)
    out_ref[:, 512:] = mul(g_ref[...], o_ref[...], NT).astype(BF16)


def both_products(n, proj, g, o):
    rows = 1152
    tall = pl.BlockSpec((rows, 256), lambda i: (i, 0))
    return pl.pallas_call(
        both_products_kernel,
        grid=(4608 // rows,),
        out_shape=jax.ShapeDtypeStruct((4608, 768), BF16),
        in_specs=[
            tall,
            pl.BlockSpec((512, 256), lambda i: (0, 0)),
            tall,
            pl.BlockSpec((256, 256), lambda i: (0, 0)),
        ],
        out_specs=pl.BlockSpec((rows, 768), lambda i: (i, 0)),
        compiler_params=params(32),
        cost_estimate=cost(2 * 4608 * 768 * 256, 12000000),
    )(n, proj, g, o)


def sided_product_kernel(flip, place_ref, n_ref, proj_ref, out_ref):
    core, x, yhi = place_ref[2], place_ref[3], place_ref[4]
    side = core if flip == 0 else 1 - core
    for ahead in range(4):
        for over in range(2):
            level = yhi if over == 0 else 1 - yhi
            slot = (level * 4 + (x + ahead) % 4) * 2 + side
            out_ref[ahead, over] = mul(n_ref[slot], proj_ref[...], NT).astype(BF16)


def sided_product(flip, place, n, proj):
    columns = proj.shape[0]
    return pl.pallas_call(
        functools.partial(sided_product_kernel, flip),
        out_shape=jax.ShapeDtypeStruct((4, 2, 288, columns), BF16),
        in_specs=[SMEM, VMEM, VMEM],
        out_specs=VMEM,
        compiler_params=params(24),
        cost_estimate=cost(2304 * 256 * 2 * columns, 5000000),
    )(place, n.reshape(16, 288, 256), proj)


def backward_kernel(routes, inputs, place_ref, qkv_ref, probs_ref, wo_ref, w_ref, *refs):
    blocks = refs[:inputs]
    proj_ref, g_ref, out_ref, wo, w, sems, w_sems = refs[inputs:]
    copies = place_blocks(routes, place_ref, blocks, [g_ref], sems)
    wo_copy = pltpu.make_async_copy(wo_ref, wo, w_sems.at[0])
    wo_copy.start()
    w_copy = pltpu.make_async_copy(w_ref, w, w_sems.at[1])
    w_copy.start()
    q, k, v = qkv_ref[:256], qkv_ref[256:384], qkv_ref[384:]
    v_rows = v.T
    for copy in copies:
        copy.wait()
    wo_copy.wait()
    d_o = mul(wo[...], g_ref[...].reshape(4608, 256), ROW).astype(BF16)
    d_k, d_v = 0.0, 0.0
    for h in range(2):
        here = slice(h * HD, (h + 1) * HD)
        d_oh = d_o[here]
        p = probs_ref[h]
        dp = mul(v_rows, d_oh, ROW)
        delta = jnp.sum(p * dp, axis=0, keepdims=True)
        ds = (p * (dp - delta) * (HD**-0.5)).astype(BF16)
        proj_ref[here] = mul(k, ds, ROW).astype(BF16)
        d_k = d_k + mul(q[here], ds, NT)
        d_v = d_v + mul(d_oh, p.astype(BF16), NT)
    proj_ref[256:384] = d_k.astype(BF16)
    proj_ref[384:] = d_v.astype(BF16)
    w_copy.wait()
    for ahead in range(8):
        depth = (place_ref[1] + ahead) % 8
        for plane in range(2):
            out_ref[ahead, plane] = mul(w[plane, depth], proj_ref[...], ROW).astype(BF16)


def backward(place, saved, routes, w_output, weights):
    qkv, probs, _ = saved
    return pl.pallas_call(
        functools.partial(backward_kernel, routes.routes, len(routes.arrays)),
        out_shape=[
            jax.ShapeDtypeStruct((512, 256), BF16),
            jax.ShapeDtypeStruct((2, 8, 288, 256), BF16),
            jax.ShapeDtypeStruct((8, 2, 288, 256), BF16),
        ],
        in_specs=[SMEM, VMEM, VMEM, ANY, ANY] + [ANY] * len(routes.arrays),
        out_specs=[VMEM] * 3,
        scratch_shapes=[
            pltpu.VMEM((256, 4608), BF16),
            pltpu.VMEM((2, 8, 288, 512), BF16),
            pltpu.SemaphoreType.DMA((len(routes.routes),)),
            pltpu.SemaphoreType.DMA((2,)),
        ],
        compiler_params=params(56),
        cost_estimate=cost(2 * 4608 * 768 * 256, 15000000),
    )(place, qkv, probs, w_output, weights.reshape(2, 8, 288, 512), *routes.arrays)


def inputs_kernel(place_ref, order_ref, assign_ref, x_ref, g_ref, gains_ref, out_ref, rows, scales, sems):
    section, shard = place_ref[5], place_ref[6]
    own = order_ref[section]
    following = order_ref[lax.rem(section + 1, 16)]
    copies = [
        pltpu.make_async_copy(gains_ref.at[assign_ref[0, 0]], scales.at[0], sems.at[0]),
        pltpu.make_async_copy(gains_ref.at[assign_ref[0, 1]], scales.at[1], sems.at[1]),
        pltpu.make_async_copy(x_ref.at[own], rows.at[0], sems.at[2]),
        pltpu.make_async_copy(x_ref.at[following], rows.at[1], sems.at[3]),
        pltpu.make_async_copy(g_ref, out_ref.at[1], sems.at[4]),
    ]
    for copy in copies:
        copy.start()
    for copy in copies:
        copy.wait()
    for number, target in ((0, 0), (1, 2)):
        line = jnp.broadcast_to(scales[number], (8, 4608))
        line = pltpu.roll(line, lax.rem(4608 - shard * 288, 4608), 1)
        column = line[:, :384].T[:288, :1]
        out_ref[target] = (rows[number].astype(F32) * column).astype(BF16)


def scaled_inputs(place, order, assign, x, g, gains):
    return pl.pallas_call(
        inputs_kernel,
        out_shape=jax.ShapeDtypeStruct((3, 288, 256), BF16),
        in_specs=[SMEM, SMEM, SMEM, ANY, ANY, ANY],
        out_specs=VMEM,
        scratch_shapes=[
            pltpu.VMEM((2, 288, 256), BF16),
            pltpu.VMEM((2, 1, 4608), F32),
            pltpu.SemaphoreType.DMA((5,)),
        ],
        compiler_params=params(16),
        cost_estimate=cost(0, 1000000),
    )(place, order, assign, x, g, gains.reshape(32, 1, 4608))


class Routes:
    def __init__(self):
        self.arrays, self.routes = [], []

    def add(self, array, pieces):
        at = len(self.arrays)
        self.arrays.append(array)
        for row, piece in enumerate(pieces):
            if piece is not None:
                self.routes.append((at, row) + piece)


def scatter_start(far):
    up = send(far[:, :144], "tensor", along_z(1))
    down = send(far[:, 144:], "tensor", along_z(-1))
    return up, down


def scatter_rest(parts, up, down, beside=()):
    up = jnp.concatenate([parts[3][:, :144] + up, parts[3][:, 144:]], axis=1)
    down = jnp.concatenate([parts[5][:, :144], parts[5][:, 144:] + down], axis=1)
    for step in (2, 1, 0):
        if beside:
            up, down, _ = lax.optimization_barrier((up, down, beside[2 - step]))
        up = send(up, "tensor", along_z(1))
        down = send(down, "tensor", along_z(-1))
        if step:
            up = parts[step] + up
            down = parts[8 - step] + down
    return parts[0].astype(F32) + up.astype(F32) + down.astype(F32)


def section_first(keep, came):
    up = send(keep[2, 0] + came[2, 0], "section", along_x(1))
    down = send(keep[2, 1] + came[2, 1], "section", along_x(-1))
    return up, down


def section_second(keep, came, up, down):
    near = keep[1] + came[1]
    up = jnp.stack([near[0] + up, near[1]])
    near = keep[3] + came[3]
    down = jnp.stack([near[0], near[1] + down])
    return send(up, "section", along_x(1)), send(down, "section", along_x(-1))


def section_third(keep, came, up, down):
    total = keep[0].astype(F32) + came[0].astype(F32) + up.astype(F32) + down.astype(F32)
    return total[0] + send(total[1].astype(BF16), "section", SWAP_YHI).astype(F32)


def forward(n, weights):
    qkv = mul(weights, n, TN).astype(BF16)
    k, v = qkv[256:384], qkv[384:]
    j = lax.broadcasted_iota(jnp.int32, (256, 256), 0)
    i = lax.broadcasted_iota(jnp.int32, (256, 256), 1)
    causal = j <= i
    probs, outs = [], []
    for h in range(2):
        scores = mul(k, qkv[h * HD : (h + 1) * HD], TN) * (HD**-0.5)
        scores = jnp.where(causal, scores, -1e30)
        top = jnp.max(scores, axis=0, keepdims=True)
        expo = jnp.where(causal, jnp.exp(scores - top), 0.0)
        p = expo / jnp.sum(expo, axis=0, keepdims=True)
        probs.append(p)
        outs.append(mul(v, p.astype(BF16), ROW).astype(BF16))
    return qkv, jnp.stack(probs), jnp.concatenate(outs, axis=0)


def body(x_saved, grad_first, gains, assign, order, w_query, w_key, w_value, w_output):
    s = lax.axis_index("section")
    t = lax.axis_index("tensor")
    z, y = t % 8, t // 8
    place = jnp.stack([y, z, s % 2, (s // 2) % 4, s // 8, s, t]).astype(jnp.int32)
    previous = [(i, (i - 1) % 16) for i in range(16)]

    def share(which, shard):
        return lax.dynamic_slice(gains, (which, shard * 288), (1, 288)).reshape(288, 1)

    full = (2, 8, 288, 256)
    plane = (8, 288, 256)

    own = scaled_inputs(
        place, order, assign, jnp.swapaxes(x_saved[0], 1, 2), grad_first[0].T, gains
    )
    other = send(own[:2], "tensor", SWAP_Y)
    ups, downs, swaps = {0: own}, {0: own}, {}
    for step in (1, 2, 3):
        up, down = ups[step - 1], downs[step - 1]
        if step == 3:
            up, down, swaps[1] = lax.optimization_barrier((up, down, swaps[1]))
        ups[step] = send(up, "tensor", along_z(1))
        downs[step] = send(down, "tensor", along_z(-1))
        swaps[step] = send(jnp.stack([downs[step][1], ups[step][1]]), "tensor", SWAP_Y)
    up, down, swaps[2] = lax.optimization_barrier((ups[3], downs[3], swaps[2]))
    far = send(up[:, :144], "tensor", along_z(1)), send(down[:, 144:], "tensor", along_z(-1))
    found_n, far_n = ring(other[:1])
    routes, g_routes = Routes(), Routes()

    def first_blocks(block, offset, half):
        routes.add(block, [(0, 0, offset, half), None, (1, None, offset, half)])
        g_routes.add(block, [None, (0, 0, offset, half)])

    first_blocks(own, 0, None)
    for step in (1, 2, 3):
        first_blocks(ups[step], -step, None)
        first_blocks(downs[step], step, None)
        g_routes.add(swaps[step], [(0, 1, step, None), (0, 1, -step, None)])
    for half in (0, 1):
        first_blocks(far[half], 4, half)
        routes.add(far_n[half], [(0, 1, 4, half)])
    swap = send(jnp.stack([far[0][1], far[1][1]]), "tensor", SWAP_Y)
    g_routes.add(swap, [(0, 1, 4, 0), (0, 1, 4, 1)])
    for offset, block in found_n.items():
        if offset:
            routes.add(block, [(0, 1, offset, None)])
    routes.add(other, [(0, 1, 0, None)])
    g_routes.add(other, [None, (0, 1, 0, None)])
    n1_full, n2_plane = assemble(routes.arrays, routes.routes, [full, plane], place)
    n1_full = n1_full.reshape(4608, 256)
    n2_other = send(n2_plane, "tensor", SWAP_Y)

    g1_next = send(own[1], "section", previous), send(other[1], "section", previous)
    g1_next = jnp.where(y == 0, g1_next[0], g1_next[1]), jnp.where(y == 0, g1_next[1], g1_next[0])
    which_next = send(assign, "section", previous)[0, 0]

    weights = jnp.concatenate([w_query, w_key, w_value], axis=1)
    saved1 = forward(n1_full, weights)
    proj1, g1_full, dn1 = backward(place, saved1, g_routes, w_output, weights)
    starts = [scatter_start(dn1[4][chain : chain + 1]) for chain in (0, 1)]

    grads1 = both_products(n1_full, proj1, g1_full.reshape(4608, 256), saved1[2])
    dn1, grads1 = lax.optimization_barrier((dn1, grads1))
    grads1 = lax.psum_scatter(grads1, "section", scatter_dimension=0, tiled=True)

    n2_full = jnp.where(
        y == 0, jnp.stack([n2_plane, n2_other]), jnp.stack([n2_other, n2_plane])
    ).reshape(4608, 256)
    saved2 = forward(n2_full, weights)
    g2 = []
    routes = Routes()
    for chain in (0, 1):
        part1 = scatter_rest(dn1[:, chain : chain + 1], *starts[chain])[0].astype(BF16)
        here = send(part1, ("section", "tensor"), to_previous(0))
        there = send(part1, ("section", "tensor"), to_previous(8))
        total = here.astype(F32) + there.astype(F32)
        scale = share(which_next, z + 8 * chain)
        shard = (g1_next[chain].astype(F32) + scale * total).astype(BF16)
        if chain == 1:
            shard, outs = lax.optimization_barrier((shard, saved2[2]))
            saved2 = saved2[:2] + (outs,)
        g2.append(shard)
        found, far = ring(shard[None])
        for offset, block in found.items():
            routes.add(block, [(0, 2 + chain, offset, None)])
        for half in (0, 1):
            routes.add(far[half], [(0, 2 + chain, 4, half)])

    saved2 = lax.optimization_barrier((saved2, grads1))
    saved2, grads1 = saved2
    proj2, g2_full, dn2 = backward(place, saved2, routes, w_output, weights)
    starts = scatter_start(dn2[4])

    g2_full = g2_full.reshape(4608, 256)
    away_l = sided_product(1, place, n2_full, proj2)
    came_l = send(away_l, "section", SWAP_CORE)
    away_r = sided_product(1, place, g2_full, saved2[2])
    came_r = send(away_r, "section", SWAP_CORE)
    keep_l = sided_product(0, place, n2_full, proj2)
    keep_r = sided_product(0, place, g2_full, saved2[2])
    first_r = section_first(keep_r, came_r)
    first_l = section_first(keep_l, came_l)
    second_r = section_second(keep_r, came_r, *first_r)
    second_l = section_second(keep_l, came_l, *first_l)
    right2 = section_third(keep_r, came_r, *second_r)
    left2 = section_third(keep_l, came_l, *second_l)

    part2 = scatter_rest(dn2, *starts, beside=((keep_l, keep_r), came_l, first_l))
    away = jnp.where(y == 0, part2[1], part2[0]).astype(BF16)
    keep = jnp.where(y == 0, part2[0], part2[1])
    dn2_own = keep + send(away, "tensor", SWAP_Y).astype(F32)
    g2_own = jnp.where(y == 0, g2[0], g2[1])
    dx2 = (g2_own.astype(F32) + share(assign[0, 1], t) * dn2_own).astype(BF16)

    left = grads1[:, :512].astype(F32) + left2
    right = grads1[:, 512:].astype(F32) + right2
    return (
        dx2.T[None],
        left[:, :256],
        left[:, 256:384],
        left[:, 384:],
        right.T,
    )


def solution(mesh):
    in_specs = (
        P("section", None, None, "tensor"),
        P("section", None, "tensor"),
        P(),
        P("section", None),
        P(),
        P(None, "tensor"),
        P(None, "tensor"),
        P(None, "tensor"),
        P("tensor", None),
    )
    out_specs = (
        P("section", None, "tensor"),
        P("section", "tensor"),
        P("section", "tensor"),
        P("section", "tensor"),
        P("tensor", "section"),
    )
    return jax.shard_map(body, mesh=mesh, in_specs=in_specs, out_specs=out_specs, check_vma=False)
```

```python
import functools

import jax
import jax.numpy as jnp
from jax import lax
from jax.experimental import pallas as pl
from jax.experimental.pallas import tpu as pltpu
from jax.sharding import PartitionSpec as P

HD = 128
F32 = jnp.float32
BF16 = jnp.bfloat16
ROW = (((1,), (0,)), ((), ()))
NT = (((1,), (1,)), ((), ()))
TN = (((0,), (0,)), ((), ()))


def mul(a, b, dims):
    return lax.dot_general(a, b, dims, preferred_element_type=F32)


def along_z(by):
    return [(t, (t & 8) | ((t + by) & 7)) for t in range(16)]


def along_x(by):
    return [(s, (s & 9) | ((((s >> 1) + by) & 3) << 1)) for s in range(16)]


SWAP_Y = [(t, t ^ 8) for t in range(16)]
SWAP_CORE = [(s, s ^ 1) for s in range(16)]
SWAP_YHI = [(s, s ^ 8) for s in range(16)]


def to_previous(flip):
    pairs = []
    for s in range(16):
        for t in range(16):
            pairs.append((s * 16 + t, ((s - 1) % 16) * 16 + (t ^ flip)))
    return pairs


def send(a, axis, pairs):
    return lax.ppermute(a, axis, pairs)


def ring(payload):
    up, down = payload, payload
    found = {0: payload}
    for step in (1, 2, 3):
        up = send(up, "tensor", along_z(1))
        down = send(down, "tensor", along_z(-1))
        found[-step] = up
        found[step] = down
    far = (
        send(up[:, :144], "tensor", along_z(1)),
        send(down[:, 144:], "tensor", along_z(-1)),
    )
    return found, far


def place_blocks(routes, place_ref, ins, outs, sems):
    copies = []
    for number, (source, row, target, plane, offset, half) in enumerate(routes):
        depth = (place_ref[1] + offset) % 8
        if plane is None:
            dst = outs[target].at[depth]
        else:
            level = (place_ref[0] + plane) % 2 if plane < 2 else plane - 2
            dst = outs[target].at[level, depth]
        if half is not None:
            dst = dst.at[pl.ds(half * 144, 144)]
        copy = pltpu.make_async_copy(ins[source].at[row], dst, sems.at[number])
        copy.start()
        copies.append(copy)
    return copies


def assemble_kernel(routes, inputs, place_ref, *refs):
    for copy in place_blocks(routes, place_ref, refs[:inputs], refs[inputs:-1], refs[-1]):
        copy.wait()


ANY = pl.BlockSpec(memory_space=pl.ANY)
SMEM = pl.BlockSpec(memory_space=pltpu.SMEM)
VMEM = pl.BlockSpec(memory_space=pltpu.VMEM)


def params(mib):
    return pltpu.CompilerParams(vmem_limit_bytes=mib * 2**20)


def cost(flops, moved):
    return pl.CostEstimate(flops=flops, bytes_accessed=moved, transcendentals=0)


def assemble(arrays, routes, out_shapes, place):
    return pl.pallas_call(
        functools.partial(assemble_kernel, routes, len(arrays)),
        out_shape=[jax.ShapeDtypeStruct(shape, BF16) for shape in out_shapes],
        in_specs=[SMEM] + [ANY] * len(arrays),
        out_specs=[VMEM] * len(out_shapes),
        scratch_shapes=[pltpu.SemaphoreType.DMA((len(routes),))],
        compiler_params=params(56),
        cost_estimate=cost(0, 10000000),
    )(place, *arrays)


def both_products_kernel(n_ref, proj_ref, g_ref, o_ref, out_ref):
    out_ref[:, :512] = mul(n_ref[...], proj_ref[...], NT).astype(BF16)
    out_ref[:, 512:] = mul(g_ref[...], o_ref[...], NT).astype(BF16)


def both_products(n, proj, g, o):
    rows = 1152
    tall = pl.BlockSpec((rows, 256), lambda i: (i, 0))
    return pl.pallas_call(
        both_products_kernel,
        grid=(4608 // rows,),
        out_shape=jax.ShapeDtypeStruct((4608, 768), BF16),
        in_specs=[
            tall,
            pl.BlockSpec((512, 256), lambda i: (0, 0)),
            tall,
            pl.BlockSpec((256, 256), lambda i: (0, 0)),
        ],
        out_specs=pl.BlockSpec((rows, 768), lambda i: (i, 0)),
        compiler_params=params(56),
        cost_estimate=cost(2 * 4608 * 768 * 256, 12000000),
    )(n, proj, g, o)


def sided_product_kernel(flip, place_ref, n_ref, proj_ref, out_ref):
    core, x, yhi = place_ref[2], place_ref[3], place_ref[4]
    side = core if flip == 0 else 1 - core
    for ahead in range(4):
        for over in range(2):
            level = yhi if over == 0 else 1 - yhi
            slot = (level * 4 + (x + ahead) % 4) * 2 + side
            out_ref[ahead, over] = mul(n_ref[slot], proj_ref[...], NT).astype(BF16)


def sided_product(flip, place, n, proj):
    columns = proj.shape[0]
    return pl.pallas_call(
        functools.partial(sided_product_kernel, flip),
        out_shape=jax.ShapeDtypeStruct((4, 2, 288, columns), BF16),
        in_specs=[SMEM, VMEM, VMEM],
        out_specs=VMEM,
        compiler_params=params(24),
        cost_estimate=cost(2304 * 256 * 2 * columns, 5000000),
    )(place, n.reshape(16, 288, 256), proj)


def backward_kernel(routes, inputs, place_ref, qkv_ref, p0_ref, p1_ref, wo_ref, w_ref, *refs):
    blocks = refs[:inputs]
    proj_ref, g_out, dn_out, g_ref, dn, wo, w, sems, w_sems, out_sems = refs[inputs:]
    copies = place_blocks(routes, place_ref, blocks, [g_ref], sems)
    wo_copy = pltpu.make_async_copy(wo_ref, wo, w_sems.at[0])
    wo_copy.start()
    w_copy = pltpu.make_async_copy(w_ref, w, w_sems.at[1])
    w_copy.start()
    q, k, v = qkv_ref[:256], qkv_ref[256:384], qkv_ref[384:]
    v_rows = v.T
    for copy in copies:
        copy.wait()
    leaving = [pltpu.make_async_copy(g_ref, g_out, out_sems.at[8])]
    leaving[0].start()
    wo_copy.wait()
    d_o = mul(wo[...], g_ref[...].reshape(4608, 256), ROW).astype(BF16)
    d_k, d_v = 0.0, 0.0
    for h in range(2):
        here = slice(h * HD, (h + 1) * HD)
        d_oh = d_o[here]
        p = (p0_ref, p1_ref)[h][...]
        dp = mul(v_rows, d_oh, ROW)
        delta = jnp.sum(p * dp, axis=0, keepdims=True)
        ds = (p * (dp - delta) * (HD**-0.5)).astype(BF16)
        proj_ref[here] = mul(k, ds, ROW).astype(BF16)
        d_k = d_k + mul(q[here], ds, NT)
        d_v = d_v + mul(d_oh, p.astype(BF16), NT)
    proj_ref[256:384] = d_k.astype(BF16)
    proj_ref[384:] = d_v.astype(BF16)
    w_copy.wait()
    proj = proj_ref[...]
    for ahead in (4, 3, 5, 2, 6, 1, 7, 0):
        depth = (place_ref[1] + ahead) % 8
        for plane in range(2):
            dn[ahead, plane] = mul(w[plane, depth], proj, ROW).astype(BF16)
        copy = pltpu.make_async_copy(dn.at[ahead], dn_out.at[ahead], out_sems.at[ahead])
        copy.start()
        leaving.append(copy)
    for copy in leaving:
        copy.wait()


def backward(place, saved, routes, w_output, weights):
    qkv, probs, _ = saved
    return pl.pallas_call(
        functools.partial(backward_kernel, routes.routes, len(routes.arrays)),
        out_shape=[
            jax.ShapeDtypeStruct((512, 256), BF16),
            jax.ShapeDtypeStruct((2, 8, 288, 256), BF16),
            jax.ShapeDtypeStruct((8, 2, 288, 256), BF16),
        ],
        in_specs=[SMEM, VMEM, VMEM, VMEM, ANY, ANY] + [ANY] * len(routes.arrays),
        out_specs=[VMEM, ANY, ANY],
        scratch_shapes=[
            pltpu.VMEM((2, 8, 288, 256), BF16),
            pltpu.VMEM((8, 2, 288, 256), BF16),
            pltpu.VMEM((256, 4608), BF16),
            pltpu.VMEM((2, 8, 288, 512), BF16),
            pltpu.SemaphoreType.DMA((len(routes.routes),)),
            pltpu.SemaphoreType.DMA((2,)),
            pltpu.SemaphoreType.DMA((9,)),
        ],
        compiler_params=params(56),
        cost_estimate=cost(2 * 4608 * 768 * 256, 15000000),
    )(place, qkv, *probs, w_output, weights.reshape(2, 8, 288, 512), *routes.arrays)


def inputs_kernel(place_ref, order_ref, assign_ref, x_ref, g_ref, gains_ref, out_ref, rows, scales, sems):
    section, shard = place_ref[5], place_ref[6]
    own = order_ref[section]
    following = order_ref[lax.rem(section + 1, 16)]
    which = assign_ref[0, 0], assign_ref[0, 1]
    groups = [pl.ds(pl.multiple_of((number // 8) * 8, 8), 8) for number in which]
    copies = [
        pltpu.make_async_copy(gains_ref.at[groups[0]], scales.at[0], sems.at[0]),
        pltpu.make_async_copy(gains_ref.at[groups[1]], scales.at[1], sems.at[1]),
        pltpu.make_async_copy(x_ref.at[own], rows.at[0], sems.at[2]),
        pltpu.make_async_copy(x_ref.at[following], rows.at[1], sems.at[3]),
        pltpu.make_async_copy(g_ref, out_ref.at[1], sems.at[4]),
    ]
    for copy in copies:
        copy.start()
    for copy in copies:
        copy.wait()
    for number, target in ((0, 0), (1, 2)):
        line = jnp.broadcast_to(scales[number, pl.ds(which[number] % 8, 1)], (8, 4608))
        line = pltpu.roll(line, lax.rem(4608 - shard * 288, 4608), 1)
        column = line[:, :384].T[:288, :1]
        out_ref[target] = (rows[number].astype(F32) * column).astype(BF16)


def scaled_inputs(place, order, assign, x, g, gains):
    return pl.pallas_call(
        inputs_kernel,
        out_shape=jax.ShapeDtypeStruct((3, 288, 256), BF16),
        in_specs=[SMEM, SMEM, SMEM, ANY, ANY, ANY],
        out_specs=VMEM,
        scratch_shapes=[
            pltpu.VMEM((2, 288, 256), BF16),
            pltpu.VMEM((2, 8, 4608), F32),
            pltpu.SemaphoreType.DMA((5,)),
        ],
        compiler_params=params(56),
        cost_estimate=cost(0, 1000000),
    )(place, order, assign, x, g, gains)


class Routes:
    def __init__(self):
        self.arrays, self.routes = [], []

    def add(self, array, pieces):
        at = len(self.arrays)
        self.arrays.append(array)
        for row, piece in enumerate(pieces):
            if piece is not None:
                self.routes.append((at, row) + piece)


def scatter_start(far):
    up = send(far[:, :144], "tensor", along_z(1))
    down = send(far[:, 144:], "tensor", along_z(-1))
    return up, down


def scatter_payload(parts, step, up, down):
    if step == 3:
        up = jnp.concatenate([parts[3][:, :144] + up, parts[3][:, 144:]], axis=1)
        down = jnp.concatenate([parts[5][:, :144], parts[5][:, 144:] + down], axis=1)
        return up, down
    return parts[step] + up, parts[8 - step] + down


def scatter_send(up, down):
    return send(up, "tensor", along_z(1)), send(down, "tensor", along_z(-1))


def scatter_total(parts, up, down):
    return parts[0].astype(F32) + up.astype(F32) + down.astype(F32)


def section_first(keep, came):
    up = send(keep[2, 0] + came[2, 0], "section", along_x(1))
    down = send(keep[2, 1] + came[2, 1], "section", along_x(-1))
    return up, down


def section_second(keep, came, up, down):
    near = keep[1] + came[1]
    up = jnp.stack([near[0] + up, near[1]])
    near = keep[3] + came[3]
    down = jnp.stack([near[0], near[1] + down])
    return send(up, "section", along_x(1)), send(down, "section", along_x(-1))


def section_third(keep, came, up, down):
    total = keep[0].astype(F32) + came[0].astype(F32) + up.astype(F32) + down.astype(F32)
    return total[0] + send(total[1].astype(BF16), "section", SWAP_YHI).astype(F32)


def forward(n, weights):
    qkv = mul(weights, n, TN).astype(BF16)
    k, v = qkv[256:384], qkv[384:]
    j = lax.broadcasted_iota(jnp.int32, (256, 256), 0)
    i = lax.broadcasted_iota(jnp.int32, (256, 256), 1)
    causal = j <= i
    probs, outs = [], []
    for h in range(2):
        scores = mul(k, qkv[h * HD : (h + 1) * HD], TN) * (HD**-0.5)
        scores = jnp.where(causal, scores, -1e30)
        top = jnp.max(scores, axis=0, keepdims=True)
        expo = jnp.where(causal, jnp.exp(scores - top), 0.0)
        p = expo / jnp.sum(expo, axis=0, keepdims=True)
        probs.append(p)
        outs.append(mul(v, p.astype(BF16), ROW).astype(BF16))
    return qkv, tuple(probs), jnp.concatenate(outs, axis=0)


def body(x_saved, grad_first, gains, assign, order, w_query, w_key, w_value, w_output):
    s = lax.axis_index("section")
    t = lax.axis_index("tensor")
    z, y = t % 8, t // 8
    place = jnp.stack([y, z, s % 2, (s // 2) % 4, s // 8, s, t]).astype(jnp.int32)
    previous = [(i, (i - 1) % 16) for i in range(16)]

    def share(which, shard):
        return lax.dynamic_slice(gains, (which, shard * 288), (1, 288)).reshape(288, 1)

    full = (2, 8, 288, 256)
    plane = (8, 288, 256)

    own = scaled_inputs(
        place, order, assign, jnp.swapaxes(x_saved[0], 1, 2), grad_first[0].T, gains
    )
    other = send(own[:2], "tensor", SWAP_Y)
    ups, downs, swaps = {0: own}, {0: own}, {}
    for step in (1, 2, 3):
        up, down = ups[step - 1], downs[step - 1]
        if step == 3:
            up, down, swaps[1] = lax.optimization_barrier((up, down, swaps[1]))
        ups[step] = send(up, "tensor", along_z(1))
        downs[step] = send(down, "tensor", along_z(-1))
        swaps[step] = send(jnp.stack([downs[step][1], ups[step][1]]), "tensor", SWAP_Y)
    up, down, swaps[2] = lax.optimization_barrier((ups[3], downs[3], swaps[2]))
    far = send(up[:, :144], "tensor", along_z(1)), send(down[:, 144:], "tensor", along_z(-1))
    found_n, far_n = ring(other[:1])
    routes, g_routes = Routes(), Routes()

    def first_blocks(block, offset, half):
        routes.add(block, [(0, 0, offset, half), None, (1, None, offset, half)])
        g_routes.add(block, [None, (0, 0, offset, half)])

    first_blocks(own, 0, None)
    for step in (1, 2, 3):
        first_blocks(ups[step], -step, None)
        first_blocks(downs[step], step, None)
        g_routes.add(swaps[step], [(0, 1, step, None), (0, 1, -step, None)])
    for half in (0, 1):
        first_blocks(far[half], 4, half)
        routes.add(far_n[half], [(0, 1, 4, half)])
    swap = send(jnp.stack([far[0][1], far[1][1]]), "tensor", SWAP_Y)
    for offset, block in found_n.items():
        if offset:
            routes.add(block, [(0, 1, offset, None)])
    routes.add(other, [(0, 1, 0, None)])
    g_routes.add(other, [None, (0, 1, 0, None)])
    n1_full, n2_plane = assemble(routes.arrays, routes.routes, [full, plane], place)
    n1_full, swap = lax.optimization_barrier((n1_full.reshape(4608, 256), swap))
    g_routes.add(swap, [(0, 1, 4, 0), (0, 1, 4, 1)])
    n2_other = send(n2_plane, "tensor", SWAP_Y)

    g1_next = send(own[1], "section", previous), send(other[1], "section", previous)
    g1_next = jnp.where(y == 0, g1_next[0], g1_next[1]), jnp.where(y == 0, g1_next[1], g1_next[0])
    which_next = send(assign, "section", previous)[0, 0]

    weights = jnp.concatenate([w_query, w_key, w_value], axis=1)
    saved1 = forward(n1_full, weights)
    proj1, g1_full, dn1 = backward(place, saved1, g_routes, w_output, weights)
    starts = [scatter_start(dn1[4][chain : chain + 1]) for chain in (0, 1)]

    proj1, starts[0] = lax.optimization_barrier((proj1, starts[0]))
    grads1 = both_products(n1_full, proj1, g1_full.reshape(4608, 256), saved1[2])
    starts[1], grads1 = lax.optimization_barrier((starts[1], grads1))
    grads1 = lax.psum_scatter(grads1, "section", scatter_dimension=0, tiled=True)

    scales = [share(which_next, z + 8 * chain) for chain in (0, 1)]
    parts = [dn1[:, chain : chain + 1] for chain in (0, 1)]
    came = [{4: starts[0]}, {4: starts[1]}]
    saved2 = None
    for step in (3, 2, 1):
        for chain in (0, 1):
            payload = scatter_payload(parts[chain], step, *came[chain][step + 1])
            if chain == 1:
                payload, came[0][step + 1] = lax.optimization_barrier((payload, came[0][step + 1]))
            elif step < 3:
                payload, came[1][step + 2] = lax.optimization_barrier((payload, came[1][step + 2]))
            if chain == 0 and step == 2:
                payload, n2_other, scales, g1_next = lax.optimization_barrier(
                    (payload, n2_other, scales, g1_next)
                )
                n2_full = jnp.where(
                    y == 0, jnp.stack([n2_plane, n2_other]), jnp.stack([n2_other, n2_plane])
                ).reshape(4608, 256)
                saved2 = forward(n2_full, weights)
            if chain == 1 and step == 1:
                payload, saved2 = lax.optimization_barrier((payload, saved2))
            came[chain][step] = scatter_send(*payload)

    g2 = []
    routes = Routes()
    for chain in (0, 1):
        part1 = scatter_total(parts[chain], *came[chain][1])[0].astype(BF16)
        here = send(part1, ("section", "tensor"), to_previous(0))
        there = send(part1, ("section", "tensor"), to_previous(8))
        total = here.astype(F32) + there.astype(F32)
        shard = (g1_next[chain].astype(F32) + scales[chain] * total).astype(BF16)
        g2.append(shard)
        found, far = ring(shard[None])
        for offset, block in found.items():
            routes.add(block, [(0, 2 + chain, offset, None)])
        for half in (0, 1):
            routes.add(far[half], [(0, 2 + chain, 4, half)])

    proj2, g2_full, dn2 = backward(place, saved2, routes, w_output, weights)
    dn2, grads1 = lax.optimization_barrier((dn2, grads1))
    step_came = scatter_start(dn2[4])

    pairs = [
        (n2_full, proj2[:256]),
        (n2_full, proj2[256:]),
        (g2_full.reshape(4608, 256), saved2[2]),
    ]
    came2 = [send(sided_product(1, place, *pair), "section", SWAP_CORE) for pair in pairs]
    keeps = [sided_product(0, place, *pair) for pair in pairs]
    firsts = [section_first(keep, there) for keep, there in zip(keeps, came2)]
    seconds = [section_second(keep, there, *first) for keep, there, first in zip(keeps, came2, firsts)]
    query2, key_value2, right2 = [
        section_third(keep, there, *second) for keep, there, second in zip(keeps, came2, seconds)
    ]

    for step in (3, 2, 1):
        payload = scatter_payload(dn2, step, *step_came)
        if step == 3:
            payload, keeps = lax.optimization_barrier((payload, keeps))
        step_came = scatter_send(*payload)
    part2 = scatter_total(dn2, *step_came)
    away = jnp.where(y == 0, part2[1], part2[0]).astype(BF16)
    keep = jnp.where(y == 0, part2[0], part2[1])
    dn2_own = keep + send(away, "tensor", SWAP_Y).astype(F32)
    g2_own = jnp.where(y == 0, g2[0], g2[1])
    dx2 = (g2_own.astype(F32) + share(assign[0, 1], t) * dn2_own).astype(BF16)

    key_value = grads1[:, 256:512].astype(F32) + key_value2
    right = grads1[:, 512:].astype(F32) + right2
    return (
        dx2.T[None],
        grads1[:, :256].astype(F32) + query2,
        key_value[:, :128],
        key_value[:, 128:],
        right.T,
    )


def solution(mesh):
    in_specs = (
        P("section", None, None, "tensor"),
        P("section", None, "tensor"),
        P(),
        P("section", None),
        P(),
        P(None, "tensor"),
        P(None, "tensor"),
        P(None, "tensor"),
        P("tensor", None),
    )
    out_specs = (
        P("section", None, "tensor"),
        P("section", "tensor"),
        P("section", "tensor"),
        P("section", "tensor"),
        P("tensor", "section"),
    )
    return jax.shard_map(body, mesh=mesh, in_specs=in_specs, out_specs=out_specs, check_vma=False)
```

```python
import functools

import jax
import jax.numpy as jnp
from jax import lax
from jax.experimental import pallas as pl
from jax.experimental.pallas import tpu as pltpu
from jax.sharding import PartitionSpec as P

HD = 128
F32 = jnp.float32
BF16 = jnp.bfloat16
ROW = (((1,), (0,)), ((), ()))
NT = (((1,), (1,)), ((), ()))
TN = (((0,), (0,)), ((), ()))


def mul(a, b, dims):
    return lax.dot_general(a, b, dims, preferred_element_type=F32)


def along_z(by):
    return [(t, (t & 8) | ((t + by) & 7)) for t in range(16)]


def along_x(by):
    return [(s, (s & 9) | ((((s >> 1) + by) & 3) << 1)) for s in range(16)]


SWAP_Y = [(t, t ^ 8) for t in range(16)]
SWAP_CORE = [(s, s ^ 1) for s in range(16)]
SWAP_YHI = [(s, s ^ 8) for s in range(16)]


def to_previous(flip):
    pairs = []
    for s in range(16):
        for t in range(16):
            pairs.append((s * 16 + t, ((s - 1) % 16) * 16 + (t ^ flip)))
    return pairs


def send(a, axis, pairs):
    return lax.ppermute(a, axis, pairs)


def ring(payload):
    up, down = payload, payload
    found = {0: payload}
    for step in (1, 2, 3):
        up = send(up, "tensor", along_z(1))
        down = send(down, "tensor", along_z(-1))
        found[-step] = up
        found[step] = down
    far = (
        send(up[:, :144], "tensor", along_z(1)),
        send(down[:, 144:], "tensor", along_z(-1)),
    )
    return found, far


def place_blocks(routes, place_ref, ins, outs, sems):
    copies = []
    for number, (source, row, target, plane, offset, half) in enumerate(routes):
        depth = (place_ref[1] + offset) % 8
        if plane is None:
            dst = outs[target].at[depth]
        else:
            level = (place_ref[0] + plane) % 2 if plane < 2 else plane - 2
            dst = outs[target].at[level, depth]
        if half is not None:
            dst = dst.at[pl.ds(half * 144, 144)]
        copy = pltpu.make_async_copy(ins[source].at[row], dst, sems.at[number])
        copy.start()
        copies.append(copy)
    return copies


def assemble_kernel(routes, inputs, place_ref, *refs):
    for copy in place_blocks(routes, place_ref, refs[:inputs], refs[inputs:-1], refs[-1]):
        copy.wait()


ANY = pl.BlockSpec(memory_space=pl.ANY)
SMEM = pl.BlockSpec(memory_space=pltpu.SMEM)
VMEM = pl.BlockSpec(memory_space=pltpu.VMEM)


def params(mib):
    return pltpu.CompilerParams(vmem_limit_bytes=mib * 2**20)


def cost(flops, moved):
    return pl.CostEstimate(flops=flops, bytes_accessed=moved, transcendentals=0)


def assemble(arrays, routes, out_shapes, place):
    return pl.pallas_call(
        functools.partial(assemble_kernel, routes, len(arrays)),
        out_shape=[jax.ShapeDtypeStruct(shape, BF16) for shape in out_shapes],
        in_specs=[SMEM] + [ANY] * len(arrays),
        out_specs=[VMEM] * len(out_shapes),
        scratch_shapes=[pltpu.SemaphoreType.DMA((len(routes),))],
        compiler_params=params(56),
        cost_estimate=cost(0, 10000000),
    )(place, *arrays)


def core_products_kernel(flip, place_ref, n_ref, proj_ref, g_ref, o_ref, *refs):
    out_ref = refs[-1]
    side = place_ref[2] if flip == 0 else 1 - place_ref[2]
    for number in range(8):
        slot = number * 2 + side
        left = mul(n_ref[slot], proj_ref[...], NT)
        right = mul(g_ref[slot], o_ref[...], NT)
        if len(refs) > 1:
            left = left + refs[0][number, :, :512].astype(F32)
            right = right + refs[0][number, :, 512:].astype(F32)
        out_ref[number, :, :512] = left.astype(BF16)
        out_ref[number, :, 512:] = right.astype(BF16)


def core_products(flip, place, n, proj, g, o, *came):
    return pl.pallas_call(
        functools.partial(core_products_kernel, flip),
        out_shape=jax.ShapeDtypeStruct((8, 288, 768), BF16),
        in_specs=[SMEM] + [VMEM] * (4 + len(came)),
        out_specs=VMEM,
        compiler_params=params(56),
        cost_estimate=cost(2304 * 768 * 2 * 256, 10000000),
    )(place, n.reshape(16, 288, 256), proj, g.reshape(16, 288, 256), o, *came)


def sided_product_kernel(flip, place_ref, n_ref, proj_ref, out_ref):
    core, x, yhi = place_ref[2], place_ref[3], place_ref[4]
    side = core if flip == 0 else 1 - core
    for ahead in range(4):
        for over in range(2):
            level = yhi if over == 0 else 1 - yhi
            slot = (level * 4 + (x + ahead) % 4) * 2 + side
            out_ref[ahead, over] = mul(n_ref[slot], proj_ref[...], NT).astype(BF16)


def sided_product(flip, place, n, proj):
    columns = proj.shape[0]
    return pl.pallas_call(
        functools.partial(sided_product_kernel, flip),
        out_shape=jax.ShapeDtypeStruct((4, 2, 288, columns), BF16),
        in_specs=[SMEM, VMEM, VMEM],
        out_specs=VMEM,
        compiler_params=params(24),
        cost_estimate=cost(2304 * 256 * 2 * columns, 5000000),
    )(place, n.reshape(16, 288, 256), proj)


def backward_kernel(routes, inputs, place_ref, qkv_ref, p0_ref, p1_ref, wo_ref, w_ref, *refs):
    blocks = refs[:inputs]
    proj_ref, g_out, dn_out, g_ref, dn, wo, w, sems, w_sems, out_sems = refs[inputs:]
    copies = place_blocks(routes, place_ref, blocks, [g_ref], sems)
    wo_copy = pltpu.make_async_copy(wo_ref, wo, w_sems.at[0])
    wo_copy.start()
    w_copy = pltpu.make_async_copy(w_ref, w, w_sems.at[1])
    w_copy.start()
    q, k, v = qkv_ref[:256], qkv_ref[256:384], qkv_ref[384:]
    v_rows = v.T
    for copy in copies:
        copy.wait()
    leaving = [pltpu.make_async_copy(g_ref, g_out, out_sems.at[2])]
    leaving[0].start()
    wo_copy.wait()
    d_o = mul(wo[...], g_ref[...].reshape(4608, 256), ROW).astype(BF16)
    d_k, d_v = 0.0, 0.0
    for h in range(2):
        here = slice(h * HD, (h + 1) * HD)
        d_oh = d_o[here]
        p = (p0_ref, p1_ref)[h][...]
        dp = mul(v_rows, d_oh, ROW)
        delta = jnp.sum(p * dp, axis=0, keepdims=True)
        ds = (p * (dp - delta) * (HD**-0.5)).astype(BF16)
        proj_ref[here] = mul(k, ds, ROW).astype(BF16)
        d_k = d_k + mul(q[here], ds, NT)
        d_v = d_v + mul(d_oh, p.astype(BF16), NT)
    proj_ref[256:384] = d_k.astype(BF16)
    proj_ref[384:] = d_v.astype(BF16)
    w_copy.wait()
    proj = proj_ref[...]
    for plane in range(2):
        part = mul(w[plane].reshape(2304, 512), proj, ROW).astype(BF16).reshape(8, 288, 256)
        for depth in range(8):
            dn[(depth + 8 - place_ref[1]) % 8, plane] = part[depth]
        copy = pltpu.make_async_copy(dn.at[:, plane], dn_out.at[:, plane], out_sems.at[plane])
        copy.start()
        leaving.append(copy)
    for copy in leaving:
        copy.wait()


def backward(place, saved, routes, w_output, weights):
    qkv, probs, _ = saved
    return pl.pallas_call(
        functools.partial(backward_kernel, routes.routes, len(routes.arrays)),
        out_shape=[
            jax.ShapeDtypeStruct((512, 256), BF16),
            jax.ShapeDtypeStruct((2, 8, 288, 256), BF16),
            jax.ShapeDtypeStruct((8, 2, 288, 256), BF16),
        ],
        in_specs=[SMEM, VMEM, VMEM, VMEM, ANY, ANY] + [ANY] * len(routes.arrays),
        out_specs=[VMEM, ANY, ANY],
        scratch_shapes=[
            pltpu.VMEM((2, 8, 288, 256), BF16),
            pltpu.VMEM((8, 2, 288, 256), BF16),
            pltpu.VMEM((256, 4608), BF16),
            pltpu.VMEM((2, 8, 288, 512), BF16),
            pltpu.SemaphoreType.DMA((len(routes.routes),)),
            pltpu.SemaphoreType.DMA((2,)),
            pltpu.SemaphoreType.DMA((3,)),
        ],
        compiler_params=params(56),
        cost_estimate=cost(2 * 4608 * 768 * 256, 15000000),
    )(place, qkv, *probs, w_output, weights.reshape(2, 8, 288, 512), *routes.arrays)


def inputs_kernel(place_ref, order_ref, assign_ref, x_ref, g_ref, gains_ref, out_ref, rows, scales, sems):
    section, shard = place_ref[5], place_ref[6]
    own = order_ref[section]
    following = order_ref[lax.rem(section + 1, 16)]
    which = assign_ref[0, 0], assign_ref[0, 1]
    groups = [pl.ds(pl.multiple_of((number // 8) * 8, 8), 8) for number in which]
    copies = [
        pltpu.make_async_copy(gains_ref.at[groups[0]], scales.at[0], sems.at[0]),
        pltpu.make_async_copy(gains_ref.at[groups[1]], scales.at[1], sems.at[1]),
        pltpu.make_async_copy(x_ref.at[own], rows.at[0], sems.at[2]),
        pltpu.make_async_copy(x_ref.at[following], rows.at[1], sems.at[3]),
        pltpu.make_async_copy(g_ref, out_ref.at[1], sems.at[4]),
    ]
    for copy in copies:
        copy.start()
    for copy in copies:
        copy.wait()
    for number, target in ((0, 0), (1, 2)):
        line = jnp.broadcast_to(scales[number, pl.ds(which[number] % 8, 1)], (8, 4608))
        line = pltpu.roll(line, lax.rem(4608 - shard * 288, 4608), 1)
        column = line[:, :384].T[:288, :1]
        out_ref[target] = (rows[number].astype(F32) * column).astype(BF16)


def scaled_inputs(place, order, assign, x, g, gains):
    return pl.pallas_call(
        inputs_kernel,
        out_shape=jax.ShapeDtypeStruct((3, 288, 256), BF16),
        in_specs=[SMEM, SMEM, SMEM, ANY, ANY, ANY],
        out_specs=VMEM,
        scratch_shapes=[
            pltpu.VMEM((2, 288, 256), BF16),
            pltpu.VMEM((2, 8, 4608), F32),
            pltpu.SemaphoreType.DMA((5,)),
        ],
        compiler_params=params(56),
        cost_estimate=cost(0, 1000000),
    )(place, order, assign, x, g, gains)


class Routes:
    def __init__(self):
        self.arrays, self.routes = [], []

    def add(self, array, pieces):
        at = len(self.arrays)
        self.arrays.append(array)
        for row, piece in enumerate(pieces):
            if piece is not None:
                self.routes.append((at, row) + piece)


def scatter_start(far):
    up = send(far[:, :144], "tensor", along_z(1))
    down = send(far[:, 144:], "tensor", along_z(-1))
    return up, down


def scatter_payload(parts, step, up, down):
    if step == 3:
        up = jnp.concatenate([parts[3][:, :144] + up, parts[3][:, 144:]], axis=1)
        down = jnp.concatenate([parts[5][:, :144], parts[5][:, 144:] + down], axis=1)
        return up, down
    return parts[step] + up, parts[8 - step] + down


def scatter_send(up, down):
    return send(up, "tensor", along_z(1)), send(down, "tensor", along_z(-1))


def scatter_total(parts, up, down):
    return parts[0].astype(F32) + up.astype(F32) + down.astype(F32)


def section_first(keep, came):
    up = send(keep[2, 0] + came[2, 0], "section", along_x(1))
    down = send(keep[2, 1] + came[2, 1], "section", along_x(-1))
    return up, down


def section_second(keep, came, up, down):
    near = keep[1] + came[1]
    up = jnp.stack([near[0] + up, near[1]])
    near = keep[3] + came[3]
    down = jnp.stack([near[0], near[1] + down])
    return send(up, "section", along_x(1)), send(down, "section", along_x(-1))


def section_third(keep, came, up, down):
    total = keep[0].astype(F32) + came[0].astype(F32) + up.astype(F32) + down.astype(F32)
    return total[0] + send(total[1].astype(BF16), "section", SWAP_YHI).astype(F32)


def forward(n, weights):
    qkv = mul(weights, n, TN).astype(BF16)
    k, v = qkv[256:384], qkv[384:]
    j = lax.broadcasted_iota(jnp.int32, (256, 256), 0)
    i = lax.broadcasted_iota(jnp.int32, (256, 256), 1)
    causal = j <= i
    probs, outs = [], []
    for h in range(2):
        scores = mul(k, qkv[h * HD : (h + 1) * HD], TN) * (HD**-0.5)
        scores = jnp.where(causal, scores, -1e30)
        top = jnp.max(scores, axis=0, keepdims=True)
        expo = jnp.where(causal, jnp.exp(scores - top), 0.0)
        p = expo / jnp.sum(expo, axis=0, keepdims=True)
        probs.append(p)
        outs.append(mul(v, p.astype(BF16), ROW).astype(BF16))
    return qkv, tuple(probs), jnp.concatenate(outs, axis=0)


def body(x_saved, grad_first, gains, assign, order, w_query, w_key, w_value, w_output):
    s = lax.axis_index("section")
    t = lax.axis_index("tensor")
    z, y = t % 8, t // 8
    place = jnp.stack([y, z, s % 2, (s // 2) % 4, s // 8, s, t]).astype(jnp.int32)
    previous = [(i, (i - 1) % 16) for i in range(16)]

    def share(which, shard):
        return lax.dynamic_slice(gains, (which, shard * 288), (1, 288)).reshape(288, 1)

    full = (2, 8, 288, 256)
    plane = (8, 288, 256)

    own = scaled_inputs(
        place, order, assign, jnp.swapaxes(x_saved[0], 1, 2), grad_first[0].T, gains
    )
    other = send(own[:2], "tensor", SWAP_Y)
    ups, downs, swaps = {0: own}, {0: own}, {}
    for step in (1, 2, 3):
        up, down = ups[step - 1], downs[step - 1]
        if step == 3:
            up, down, swaps[1] = lax.optimization_barrier((up, down, swaps[1]))
        ups[step] = send(up, "tensor", along_z(1))
        downs[step] = send(down, "tensor", along_z(-1))
        swaps[step] = send(jnp.stack([downs[step][1], ups[step][1]]), "tensor", SWAP_Y)
    up, down, swaps[2] = lax.optimization_barrier((ups[3], downs[3], swaps[2]))
    far = send(up[:, :144], "tensor", along_z(1)), send(down[:, 144:], "tensor", along_z(-1))
    found_n, far_n = ring(other[:1])
    routes, g_routes = Routes(), Routes()

    def first_blocks(block, offset, half):
        routes.add(block, [(0, 0, offset, half), None, (1, None, offset, half)])
        g_routes.add(block, [None, (0, 0, offset, half)])

    first_blocks(own, 0, None)
    for step in (1, 2, 3):
        first_blocks(ups[step], -step, None)
        first_blocks(downs[step], step, None)
        g_routes.add(swaps[step], [(0, 1, step, None), (0, 1, -step, None)])
    for half in (0, 1):
        first_blocks(far[half], 4, half)
        routes.add(far_n[half], [(0, 1, 4, half)])
    swap = send(jnp.stack([far[0][1], far[1][1]]), "tensor", SWAP_Y)
    for offset, block in found_n.items():
        if offset:
            routes.add(block, [(0, 1, offset, None)])
    routes.add(other, [(0, 1, 0, None)])
    g_routes.add(other, [None, (0, 1, 0, None)])
    n1_full, n2_plane = assemble(routes.arrays, routes.routes, [full, plane], place)
    n1_full, swap = lax.optimization_barrier((n1_full.reshape(4608, 256), swap))
    g_routes.add(swap, [(0, 1, 4, 0), (0, 1, 4, 1)])
    n2_other = send(n2_plane, "tensor", SWAP_Y)

    g1_next = send(own[1], "section", previous), send(other[1], "section", previous)
    g1_next = jnp.where(y == 0, g1_next[0], g1_next[1]), jnp.where(y == 0, g1_next[1], g1_next[0])
    which_next = send(assign, "section", previous)[0, 0]

    weights = jnp.concatenate([w_query, w_key, w_value], axis=1)
    saved1 = forward(n1_full, weights)
    proj1, g1_full, dn1 = backward(place, saved1, g_routes, w_output, weights)
    starts = [scatter_start(dn1[4][chain : chain + 1]) for chain in (0, 1)]

    proj1, starts[0] = lax.optimization_barrier((proj1, starts[0]))
    factors = place, n1_full, proj1, g1_full, saved1[2]
    grads1 = send(core_products(1, *factors), "section", SWAP_CORE)

    scales = [share(which_next, z + 8 * chain) for chain in (0, 1)]
    parts = [dn1[:, chain : chain + 1] for chain in (0, 1)]
    came = [{4: starts[0]}, {4: starts[1]}]
    saved2 = None
    for step in (3, 2, 1):
        for chain in (0, 1):
            payload = scatter_payload(parts[chain], step, *came[chain][step + 1])
            if chain == 1:
                payload, came[0][step + 1] = lax.optimization_barrier((payload, came[0][step + 1]))
            elif step < 3:
                payload, came[1][step + 2] = lax.optimization_barrier((payload, came[1][step + 2]))
            if chain == 0 and step == 2:
                payload, n2_other, scales, g1_next = lax.optimization_barrier(
                    (payload, n2_other, scales, g1_next)
                )
                n2_full = jnp.where(
                    y == 0, jnp.stack([n2_plane, n2_other]), jnp.stack([n2_other, n2_plane])
                ).reshape(4608, 256)
                saved2 = forward(n2_full, weights)
            if chain == 1 and step == 2:
                grads1 = core_products(0, *factors, grads1)
                payload, grads1 = lax.optimization_barrier((payload, grads1))
            if chain == 1 and step == 1:
                payload, saved2 = lax.optimization_barrier((payload, saved2))
            came[chain][step] = scatter_send(*payload)

    grads1 = lax.psum_scatter(
        grads1.reshape(2304, 768),
        "section",
        scatter_dimension=0,
        axis_index_groups=[list(range(0, 16, 2)), list(range(1, 16, 2))],
        tiled=True,
    )

    g2 = []
    routes = Routes()
    for chain in (0, 1):
        part1 = scatter_total(parts[chain], *came[chain][1])[0].astype(BF16)
        here = send(part1, ("section", "tensor"), to_previous(0))
        there = send(part1, ("section", "tensor"), to_previous(8))
        total = here.astype(F32) + there.astype(F32)
        shard = (g1_next[chain].astype(F32) + scales[chain] * total).astype(BF16)
        g2.append(shard)
        found, far = ring(shard[None])
        for offset, block in found.items():
            routes.add(block, [(0, 2 + chain, offset, None)])
        for half in (0, 1):
            routes.add(far[half], [(0, 2 + chain, 4, half)])

    proj2, g2_full, dn2 = backward(place, saved2, routes, w_output, weights)
    dn2, grads1 = lax.optimization_barrier((dn2, grads1))
    step_came = scatter_start(dn2[4])

    pairs = [
        (n2_full, proj2[:256]),
        (n2_full, proj2[256:]),
        (g2_full.reshape(4608, 256), saved2[2]),
    ]
    came2 = [send(sided_product(1, place, *pair), "section", SWAP_CORE) for pair in pairs]
    keeps = [sided_product(0, place, *pair) for pair in pairs]
    def tie(value, *others):
        return lax.optimization_barrier((value,) + others)

    step_came, keeps = tie(step_came, keeps)
    step2 = scatter_send(*scatter_payload(dn2, 3, *step_came))
    first0 = section_first(keeps[0], came2[0])
    came2[1], first0 = tie(came2[1], first0)
    first1 = section_first(keeps[1], came2[1])
    came2[2], first0, step2 = tie(came2[2], first0, step2)
    first2 = section_first(keeps[2], came2[2])
    payload, first1 = tie(scatter_payload(dn2, 2, *step2), first1)
    step3 = scatter_send(*payload)
    second0 = section_second(keeps[0], came2[0], *first0)
    first1, first2 = tie(first1, first2)
    second1 = section_second(keeps[1], came2[1], *first1)
    payload, first2 = tie(scatter_payload(dn2, 1, *step3), first2)
    step_came = scatter_send(*payload)
    first2, step3 = tie(first2, step3)
    second2 = section_second(keeps[2], came2[2], *first2)
    query2, key_value2, right2 = [
        section_third(keep, there, *second)
        for keep, there, second in zip(keeps, came2, (second0, second1, second2))
    ]

    part2 = scatter_total(dn2, *step_came)
    away = jnp.where(y == 0, part2[1], part2[0]).astype(BF16)
    keep = jnp.where(y == 0, part2[0], part2[1])
    dn2_own = keep + send(away, "tensor", SWAP_Y).astype(F32)
    g2_own = jnp.where(y == 0, g2[0], g2[1])
    dx2 = (g2_own.astype(F32) + share(assign[0, 1], t) * dn2_own).astype(BF16)

    key_value = grads1[:, 256:512].astype(F32) + key_value2
    right = grads1[:, 512:].astype(F32) + right2
    return (
        dx2.T[None],
        grads1[:, :256].astype(F32) + query2,
        key_value[:, :128],
        key_value[:, 128:],
        right.T,
    )


def solution(mesh):
    in_specs = (
        P("section", None, None, "tensor"),
        P("section", None, "tensor"),
        P(),
        P("section", None),
        P(),
        P(None, "tensor"),
        P(None, "tensor"),
        P(None, "tensor"),
        P("tensor", None),
    )
    out_specs = (
        P("section", None, "tensor"),
        P("section", "tensor"),
        P("section", "tensor"),
        P("section", "tensor"),
        P("tensor", "section"),
    )
    return jax.shard_map(body, mesh=mesh, in_specs=in_specs, out_specs=out_specs, check_vma=False)
```

```python
import functools

import jax
import jax.numpy as jnp
from jax import lax
from jax.experimental import pallas as pl
from jax.experimental.pallas import tpu as pltpu
from jax.sharding import PartitionSpec as P

HD = 128
F32 = jnp.float32
BF16 = jnp.bfloat16
ROW = (((1,), (0,)), ((), ()))
NT = (((1,), (1,)), ((), ()))
TN = (((0,), (0,)), ((), ()))


def mul(a, b, dims):
    return lax.dot_general(a, b, dims, preferred_element_type=F32)


def along_z(by):
    return [(t, (t & 8) | ((t + by) & 7)) for t in range(16)]


def along_x(by):
    return [(s, (s & 9) | ((((s >> 1) + by) & 3) << 1)) for s in range(16)]


SWAP_Y = [(t, t ^ 8) for t in range(16)]
SWAP_CORE = [(s, s ^ 1) for s in range(16)]
SWAP_YHI = [(s, s ^ 8) for s in range(16)]


def to_previous(flip):
    pairs = []
    for s in range(16):
        for t in range(16):
            pairs.append((s * 16 + t, ((s - 1) % 16) * 16 + (t ^ flip)))
    return pairs


def send(a, axis, pairs):
    return lax.ppermute(a, axis, pairs)


def ring(payload):
    up, down = payload, payload
    found = {0: payload}
    for step in (1, 2, 3):
        up = send(up, "tensor", along_z(1))
        down = send(down, "tensor", along_z(-1))
        found[-step] = up
        found[step] = down
    far = (
        send(up[:, :144], "tensor", along_z(1)),
        send(down[:, 144:], "tensor", along_z(-1)),
    )
    return found, far


def place_blocks(routes, place_ref, ins, outs, sems):
    copies = []
    for number, (source, row, target, plane, offset, half) in enumerate(routes):
        depth = (place_ref[1] + offset) % 8
        if plane is None:
            dst = outs[target].at[depth]
        else:
            level = (place_ref[0] + plane) % 2 if plane < 2 else plane - 2
            dst = outs[target].at[level, depth]
        if half is not None:
            dst = dst.at[pl.ds(half * 144, 144)]
        copy = pltpu.make_async_copy(ins[source].at[row], dst, sems.at[number])
        copy.start()
        copies.append(copy)
    return copies


def assemble_kernel(routes, inputs, place_ref, *refs):
    for copy in place_blocks(routes, place_ref, refs[:inputs], refs[inputs:-1], refs[-1]):
        copy.wait()


ANY = pl.BlockSpec(memory_space=pl.ANY)
SMEM = pl.BlockSpec(memory_space=pltpu.SMEM)
VMEM = pl.BlockSpec(memory_space=pltpu.VMEM)


def params(mib):
    return pltpu.CompilerParams(vmem_limit_bytes=mib * 2**20)


def cost(flops, moved):
    return pl.CostEstimate(flops=flops, bytes_accessed=moved, transcendentals=0)


def assemble(arrays, routes, out_shapes, place):
    return pl.pallas_call(
        functools.partial(assemble_kernel, routes, len(arrays)),
        out_shape=[jax.ShapeDtypeStruct(shape, BF16) for shape in out_shapes],
        in_specs=[SMEM] + [ANY] * len(arrays),
        out_specs=[VMEM] * len(out_shapes),
        scratch_shapes=[pltpu.SemaphoreType.DMA((len(routes),))],
        compiler_params=params(56),
        cost_estimate=cost(0, 10000000),
    )(place, *arrays)


def both_products_kernel(n_ref, proj_ref, g_ref, o_ref, out_ref):
    out_ref[:, :512] = mul(n_ref[...], proj_ref[...], NT).astype(BF16)
    out_ref[:, 512:] = mul(g_ref[...], o_ref[...], NT).astype(BF16)


def both_products(n, proj, g, o):
    rows = 1152
    tall = pl.BlockSpec((rows, 256), lambda i: (i, 0))
    return pl.pallas_call(
        both_products_kernel,
        grid=(4608 // rows,),
        out_shape=jax.ShapeDtypeStruct((4608, 768), BF16),
        in_specs=[
            tall,
            pl.BlockSpec((512, 256), lambda i: (0, 0)),
            tall,
            pl.BlockSpec((256, 256), lambda i: (0, 0)),
        ],
        out_specs=pl.BlockSpec((rows, 768), lambda i: (i, 0)),
        compiler_params=params(56),
        cost_estimate=cost(2 * 4608 * 768 * 256, 12000000),
    )(n, proj, g, o)


def sided_products_kernel(flip, count, place_ref, *refs):
    pairs, out_ref = [refs[2 * i : 2 * i + 2] for i in range(count)], refs[-1]
    core, x, yhi = place_ref[2], place_ref[3], place_ref[4]
    side = core if flip == 0 else 1 - core
    for ahead in range(4):
        for over in range(2):
            level = yhi if over == 0 else 1 - yhi
            slot = (level * 4 + (x + ahead) % 4) * 2 + side
            at = 0
            for n_ref, proj_ref in pairs:
                columns = proj_ref.shape[0]
                part = mul(n_ref[slot], proj_ref[...], NT).astype(BF16)
                out_ref[ahead, over, :, at : at + columns] = part
                at += columns


def sided_products(flip, place, pairs):
    columns = sum(proj.shape[0] for _, proj in pairs)
    return pl.pallas_call(
        functools.partial(sided_products_kernel, flip, len(pairs)),
        out_shape=jax.ShapeDtypeStruct((4, 2, 288, columns), BF16),
        in_specs=[SMEM] + [VMEM] * (2 * len(pairs)),
        out_specs=VMEM,
        compiler_params=params(24),
        cost_estimate=cost(2304 * 256 * 2 * columns, 5000000),
    )(place, *[part for n, proj in pairs for part in (n.reshape(16, 288, 256), proj)])


def backward_kernel(routes, inputs, place_ref, qkv_ref, p0_ref, p1_ref, wo_ref, w_ref, *refs):
    blocks = refs[:inputs]
    proj_ref, g_out, dn_out, g_ref, dn, wo, w, sems, w_sems, out_sems = refs[inputs:]
    copies = place_blocks(routes, place_ref, blocks, [g_ref], sems)
    wo_copy = pltpu.make_async_copy(wo_ref, wo, w_sems.at[0])
    wo_copy.start()
    w_copy = pltpu.make_async_copy(w_ref, w, w_sems.at[1])
    w_copy.start()
    q, k, v = qkv_ref[:256], qkv_ref[256:384], qkv_ref[384:]
    v_rows = v.T
    for copy in copies:
        copy.wait()
    leaving = [pltpu.make_async_copy(g_ref, g_out, out_sems.at[2])]
    leaving[0].start()
    wo_copy.wait()
    d_o = mul(wo[...], g_ref[...].reshape(4608, 256), ROW).astype(BF16)
    d_k, d_v = 0.0, 0.0
    for h in range(2):
        here = slice(h * HD, (h + 1) * HD)
        d_oh = d_o[here]
        p = (p0_ref, p1_ref)[h][...]
        dp = mul(v_rows, d_oh, ROW)
        delta = jnp.sum(p * dp, axis=0, keepdims=True)
        ds = (p * (dp - delta) * (HD**-0.5)).astype(BF16)
        proj_ref[here] = mul(k, ds, ROW).astype(BF16)
        d_k = d_k + mul(q[here], ds, NT)
        d_v = d_v + mul(d_oh, p.astype(BF16), NT)
    proj_ref[256:384] = d_k.astype(BF16)
    proj_ref[384:] = d_v.astype(BF16)
    w_copy.wait()
    proj = proj_ref[...]
    for plane in range(2):
        part = mul(w[plane].reshape(2304, 512), proj, ROW).astype(BF16).reshape(8, 288, 256)
        for depth in range(8):
            dn[(depth + 8 - place_ref[1]) % 8, plane] = part[depth]
        copy = pltpu.make_async_copy(dn.at[:, plane], dn_out.at[:, plane], out_sems.at[plane])
        copy.start()
        leaving.append(copy)
    for copy in leaving:
        copy.wait()


def backward(place, saved, routes, w_output, weights):
    qkv, probs, _ = saved
    return pl.pallas_call(
        functools.partial(backward_kernel, routes.routes, len(routes.arrays)),
        out_shape=[
            jax.ShapeDtypeStruct((512, 256), BF16),
            jax.ShapeDtypeStruct((2, 8, 288, 256), BF16),
            jax.ShapeDtypeStruct((8, 2, 288, 256), BF16),
        ],
        in_specs=[SMEM, VMEM, VMEM, VMEM, ANY, ANY] + [ANY] * len(routes.arrays),
        out_specs=[VMEM, ANY, ANY],
        scratch_shapes=[
            pltpu.VMEM((2, 8, 288, 256), BF16),
            pltpu.VMEM((8, 2, 288, 256), BF16),
            pltpu.VMEM((256, 4608), BF16),
            pltpu.VMEM((2, 8, 288, 512), BF16),
            pltpu.SemaphoreType.DMA((len(routes.routes),)),
            pltpu.SemaphoreType.DMA((2,)),
            pltpu.SemaphoreType.DMA((3,)),
        ],
        compiler_params=params(56),
        cost_estimate=cost(2 * 4608 * 768 * 256, 15000000),
    )(place, qkv, *probs, w_output, weights.reshape(2, 8, 288, 512), *routes.arrays)


def inputs_kernel(place_ref, order_ref, assign_ref, x_ref, g_ref, gains_ref, out_ref, rows, scales, sems):
    section, shard = place_ref[5], place_ref[6]
    own = order_ref[section]
    following = order_ref[lax.rem(section + 1, 16)]
    which = assign_ref[0, 0], assign_ref[0, 1]
    groups = [pl.ds(pl.multiple_of((number // 8) * 8, 8), 8) for number in which]
    copies = [
        pltpu.make_async_copy(gains_ref.at[groups[0]], scales.at[0], sems.at[0]),
        pltpu.make_async_copy(gains_ref.at[groups[1]], scales.at[1], sems.at[1]),
        pltpu.make_async_copy(x_ref.at[own], rows.at[0], sems.at[2]),
        pltpu.make_async_copy(x_ref.at[following], rows.at[1], sems.at[3]),
        pltpu.make_async_copy(g_ref, out_ref.at[1], sems.at[4]),
    ]
    for copy in copies:
        copy.start()
    for copy in copies:
        copy.wait()
    for number, target in ((0, 0), (1, 2)):
        line = jnp.broadcast_to(scales[number, pl.ds(which[number] % 8, 1)], (8, 4608))
        line = pltpu.roll(line, lax.rem(4608 - shard * 288, 4608), 1)
        column = line[:, :384].T[:288, :1]
        out_ref[target] = (rows[number].astype(F32) * column).astype(BF16)


def scaled_inputs(place, order, assign, x, g, gains):
    return pl.pallas_call(
        inputs_kernel,
        out_shape=jax.ShapeDtypeStruct((3, 288, 256), BF16),
        in_specs=[SMEM, SMEM, SMEM, ANY, ANY, ANY],
        out_specs=VMEM,
        scratch_shapes=[
            pltpu.VMEM((2, 288, 256), BF16),
            pltpu.VMEM((2, 8, 4608), F32),
            pltpu.SemaphoreType.DMA((5,)),
        ],
        compiler_params=params(56),
        cost_estimate=cost(0, 1000000),
    )(place, order, assign, x, g, gains)


class Routes:
    def __init__(self):
        self.arrays, self.routes = [], []

    def add(self, array, pieces):
        at = len(self.arrays)
        self.arrays.append(array)
        for row, piece in enumerate(pieces):
            if piece is not None:
                self.routes.append((at, row) + piece)


def scatter_start(far):
    up = send(far[:, :144], "tensor", along_z(1))
    down = send(far[:, 144:], "tensor", along_z(-1))
    return up, down


def scatter_payload(parts, step, up, down):
    if step == 3:
        up = jnp.concatenate([parts[3][:, :144] + up, parts[3][:, 144:]], axis=1)
        down = jnp.concatenate([parts[5][:, :144], parts[5][:, 144:] + down], axis=1)
        return up, down
    return parts[step] + up, parts[8 - step] + down


def scatter_send(up, down):
    return send(up, "tensor", along_z(1)), send(down, "tensor", along_z(-1))


def scatter_total(parts, up, down):
    return parts[0].astype(F32) + up.astype(F32) + down.astype(F32)


def section_first(keep, came):
    up = send(keep[2, 0] + came[2, 0], "section", along_x(1))
    down = send(keep[2, 1] + came[2, 1], "section", along_x(-1))
    return up, down


def section_second(keep, came, up, down):
    near = keep[1] + came[1]
    up = jnp.stack([near[0] + up, near[1]])
    near = keep[3] + came[3]
    down = jnp.stack([near[0], near[1] + down])
    return send(up, "section", along_x(1)), send(down, "section", along_x(-1))


def section_third(keep, came, up, down):
    total = keep[0].astype(F32) + came[0].astype(F32) + up.astype(F32) + down.astype(F32)
    return total[0] + send(total[1].astype(BF16), "section", SWAP_YHI).astype(F32)


def forward(n, weights):
    qkv = mul(weights, n, TN).astype(BF16)
    k, v = qkv[256:384], qkv[384:]
    j = lax.broadcasted_iota(jnp.int32, (256, 256), 0)
    i = lax.broadcasted_iota(jnp.int32, (256, 256), 1)
    causal = j <= i
    probs, outs = [], []
    for h in range(2):
        scores = mul(k, qkv[h * HD : (h + 1) * HD], TN) * (HD**-0.5)
        scores = jnp.where(causal, scores, -1e30)
        top = jnp.max(scores, axis=0, keepdims=True)
        expo = jnp.where(causal, jnp.exp(scores - top), 0.0)
        p = expo / jnp.sum(expo, axis=0, keepdims=True)
        probs.append(p)
        outs.append(mul(v, p.astype(BF16), ROW).astype(BF16))
    return qkv, tuple(probs), jnp.concatenate(outs, axis=0)


def tie(value, *others):
    return lax.optimization_barrier((value,) + others)


def body(x_saved, grad_first, gains, assign, order, w_query, w_key, w_value, w_output):
    s = lax.axis_index("section")
    t = lax.axis_index("tensor")
    z, y = t % 8, t // 8
    place = jnp.stack([y, z, s % 2, (s // 2) % 4, s // 8, s, t]).astype(jnp.int32)
    previous = [(i, (i - 1) % 16) for i in range(16)]

    def share(which, shard):
        return lax.dynamic_slice(gains, (which, shard * 288), (1, 288)).reshape(288, 1)

    full = (2, 8, 288, 256)
    plane = (8, 288, 256)

    own = scaled_inputs(
        place, order, assign, jnp.swapaxes(x_saved[0], 1, 2), grad_first[0].T, gains
    )
    other = send(own[:2], "tensor", SWAP_Y)
    ups, downs, swaps = {0: own}, {0: own}, {}
    for step in (1, 2, 3):
        up, down = ups[step - 1], downs[step - 1]
        if step == 3:
            up, down, swaps[1] = lax.optimization_barrier((up, down, swaps[1]))
        ups[step] = send(up, "tensor", along_z(1))
        downs[step] = send(down, "tensor", along_z(-1))
        swaps[step] = send(jnp.stack([downs[step][1], ups[step][1]]), "tensor", SWAP_Y)
    up, down, swaps[2] = lax.optimization_barrier((ups[3], downs[3], swaps[2]))
    far = send(up[:, :144], "tensor", along_z(1)), send(down[:, 144:], "tensor", along_z(-1))
    found_n, far_n = ring(other[:1])
    routes, g_routes = Routes(), Routes()

    def first_blocks(block, offset, half):
        routes.add(block, [(0, 0, offset, half), None, (1, None, offset, half)])
        g_routes.add(block, [None, (0, 0, offset, half)])

    first_blocks(own, 0, None)
    for step in (1, 2, 3):
        first_blocks(ups[step], -step, None)
        first_blocks(downs[step], step, None)
        g_routes.add(swaps[step], [(0, 1, step, None), (0, 1, -step, None)])
    for half in (0, 1):
        first_blocks(far[half], 4, half)
        routes.add(far_n[half], [(0, 1, 4, half)])
    swap = send(jnp.stack([far[0][1], far[1][1]]), "tensor", SWAP_Y)
    for offset, block in found_n.items():
        if offset:
            routes.add(block, [(0, 1, offset, None)])
    routes.add(other, [(0, 1, 0, None)])
    g_routes.add(other, [None, (0, 1, 0, None)])
    n1_full, n2_plane = assemble(routes.arrays, routes.routes, [full, plane], place)
    n1_full, swap = lax.optimization_barrier((n1_full.reshape(4608, 256), swap))
    g_routes.add(swap, [(0, 1, 4, 0), (0, 1, 4, 1)])
    n2_other = send(n2_plane, "tensor", SWAP_Y)

    g1_next = send(own[1], "section", previous), send(other[1], "section", previous)
    g1_next = jnp.where(y == 0, g1_next[0], g1_next[1]), jnp.where(y == 0, g1_next[1], g1_next[0])
    which_next = send(assign, "section", previous)[0, 0]

    weights = jnp.concatenate([w_query, w_key, w_value], axis=1)
    saved1 = forward(n1_full, weights)
    proj1, g1_full, dn1 = backward(place, saved1, g_routes, w_output, weights)
    scales = jnp.stack([share(which_next, z + 8 * chain) for chain in (0, 1)])
    came = scatter_start(dn1[4])
    proj1, came = tie(proj1, came)
    came = scatter_send(*scatter_payload(dn1, 3, *came))
    grads1 = both_products(n1_full, proj1, g1_full.reshape(4608, 256), saved1[2])
    payload, grads1, n2_other, scales, g1_next = tie(
        scatter_payload(dn1, 2, *came), grads1, n2_other, scales, g1_next
    )
    came = scatter_send(*payload)
    grads1 = lax.psum_scatter(grads1, "section", scatter_dimension=0, tiled=True)
    n2_full = jnp.where(
        y == 0, jnp.stack([n2_plane, n2_other]), jnp.stack([n2_other, n2_plane])
    ).reshape(4608, 256)
    saved2 = forward(n2_full, weights)
    payload, saved2 = tie(scatter_payload(dn1, 1, *came), saved2)
    came = scatter_send(*payload)
    part1 = scatter_total(dn1, *came).astype(BF16)
    here = send(part1, ("section", "tensor"), to_previous(0))
    there = send(part1, ("section", "tensor"), to_previous(8))

    g2 = []
    routes = Routes()
    for chain in (0, 1):
        total = here[chain].astype(F32) + there[chain].astype(F32)
        shard = (g1_next[chain].astype(F32) + scales[chain] * total).astype(BF16)
        g2.append(shard)
        found, far = ring(shard[None])
        for offset, block in found.items():
            routes.add(block, [(0, 2 + chain, offset, None)])
        for half in (0, 1):
            routes.add(far[half], [(0, 2 + chain, 4, half)])

    proj2, g2_full, dn2 = backward(place, saved2, routes, w_output, weights)
    step_came = scatter_start(dn2[4])

    g2_full = g2_full.reshape(4608, 256)

    def pairs(proj):
        return [(n2_full, proj[:384])], [(n2_full, proj[384:]), (g2_full, saved2[2])]

    came2 = [send(sided_products(1, place, pair), "section", SWAP_CORE) for pair in pairs(proj2)]
    proj2, step_came = tie(proj2, step_came)
    keeps = [sided_products(0, place, pair) for pair in pairs(proj2)]
    step2 = scatter_send(*scatter_payload(dn2, 3, *step_came))
    first0 = section_first(keeps[0], came2[0])
    came2[1], step2 = tie(came2[1], step2)
    first1 = section_first(keeps[1], came2[1])
    payload, first0, grads1 = tie(scatter_payload(dn2, 2, *step2), first0, grads1)
    step3 = scatter_send(*payload)
    second0 = section_second(keeps[0], came2[0], *first0)
    payload, first1 = tie(scatter_payload(dn2, 1, *step3), first1)
    step_came = scatter_send(*payload)
    first1, step3 = tie(first1, step3)
    second1 = section_second(keeps[1], came2[1], *first1)
    last0, last1 = [
        section_third(keep, there, *second)
        for keep, there, second in zip(keeps, came2, (second0, second1))
    ]

    part2 = scatter_total(dn2, *step_came)
    away = jnp.where(y == 0, part2[1], part2[0]).astype(BF16)
    keep = jnp.where(y == 0, part2[0], part2[1])
    dn2_own = keep + send(away, "tensor", SWAP_Y).astype(F32)
    g2_own = jnp.where(y == 0, g2[0], g2[1])
    dx2 = (g2_own.astype(F32) + share(assign[0, 1], t) * dn2_own).astype(BF16)

    left = grads1[:, :384].astype(F32) + last0
    right = grads1[:, 384:].astype(F32) + last1
    return (
        dx2.T[None],
        left[:, :256],
        left[:, 256:],
        right[:, :128],
        right[:, 128:].T,
    )


def solution(mesh):
    in_specs = (
        P("section", None, None, "tensor"),
        P("section", None, "tensor"),
        P(),
        P("section", None),
        P(),
        P(None, "tensor"),
        P(None, "tensor"),
        P(None, "tensor"),
        P("tensor", None),
    )
    out_specs = (
        P("section", None, "tensor"),
        P("section", "tensor"),
        P("section", "tensor"),
        P("section", "tensor"),
        P("tensor", "section"),
    )
    return jax.shard_map(body, mesh=mesh, in_specs=in_specs, out_specs=out_specs, check_vma=False)
```

```python
import functools

import jax
import jax.numpy as jnp
from jax import lax
from jax.experimental import pallas as pl
from jax.experimental.pallas import tpu as pltpu
from jax.sharding import PartitionSpec as P

HD = 128
F32 = jnp.float32
BF16 = jnp.bfloat16
ROW = (((1,), (0,)), ((), ()))
NT = (((1,), (1,)), ((), ()))
TN = (((0,), (0,)), ((), ()))


def mul(a, b, dims):
    return lax.dot_general(a, b, dims, preferred_element_type=F32)


def along_z(by):
    return [(t, (t & 8) | ((t + by) & 7)) for t in range(16)]


def along_x(by):
    return [(s, (s & 9) | ((((s >> 1) + by) & 3) << 1)) for s in range(16)]


SWAP_Y = [(t, t ^ 8) for t in range(16)]
SWAP_CORE = [(s, s ^ 1) for s in range(16)]
SWAP_YHI = [(s, s ^ 8) for s in range(16)]


def to_previous(flip):
    pairs = []
    for s in range(16):
        for t in range(16):
            pairs.append((s * 16 + t, ((s - 1) % 16) * 16 + (t ^ flip)))
    return pairs


def send(a, axis, pairs):
    return lax.ppermute(a, axis, pairs)


def ring(payload):
    up, down = payload, payload
    found = {0: payload}
    for step in (1, 2, 3):
        up = send(up, "tensor", along_z(1))
        down = send(down, "tensor", along_z(-1))
        found[-step] = up
        found[step] = down
    far = (
        send(up[:, :144], "tensor", along_z(1)),
        send(down[:, 144:], "tensor", along_z(-1)),
    )
    return found, far


def place_blocks(routes, place_ref, ins, outs, sems):
    copies = []
    for number, (source, row, target, plane, offset, half) in enumerate(routes):
        depth = (place_ref[1] + offset) % 8
        if plane is None:
            dst = outs[target].at[depth]
        else:
            level = (place_ref[0] + plane) % 2 if plane < 2 else plane - 2
            dst = outs[target].at[level, depth]
        if half is not None:
            dst = dst.at[pl.ds(half * 144, 144)]
        copy = pltpu.make_async_copy(ins[source].at[row], dst, sems.at[number])
        copy.start()
        copies.append(copy)
    return copies


def assemble_kernel(routes, inputs, place_ref, *refs):
    for copy in place_blocks(routes, place_ref, refs[:inputs], refs[inputs:-1], refs[-1]):
        copy.wait()


ANY = pl.BlockSpec(memory_space=pl.ANY)
SMEM = pl.BlockSpec(memory_space=pltpu.SMEM)
VMEM = pl.BlockSpec(memory_space=pltpu.VMEM)


def params(mib):
    return pltpu.CompilerParams(vmem_limit_bytes=mib * 2**20)


def cost(flops, moved):
    return pl.CostEstimate(flops=flops, bytes_accessed=moved, transcendentals=0)


def assemble(arrays, routes, out_shapes, place):
    return pl.pallas_call(
        functools.partial(assemble_kernel, routes, len(arrays)),
        out_shape=[jax.ShapeDtypeStruct(shape, BF16) for shape in out_shapes],
        in_specs=[SMEM] + [ANY] * len(arrays),
        out_specs=[VMEM] * len(out_shapes),
        scratch_shapes=[pltpu.SemaphoreType.DMA((len(routes),))],
        compiler_params=params(56),
        cost_estimate=cost(0, 10000000),
    )(place, *arrays)


def both_products_kernel(n_ref, proj_ref, g_ref, o_ref, out_ref):
    out_ref[:, :512] = mul(n_ref[...], proj_ref[...], NT).astype(BF16)
    out_ref[:, 512:] = mul(g_ref[...], o_ref[...], NT).astype(BF16)


def both_products(n, proj, g, o):
    rows = 1152
    tall = pl.BlockSpec((rows, 256), lambda i: (i, 0))
    return pl.pallas_call(
        both_products_kernel,
        grid=(4608 // rows,),
        out_shape=jax.ShapeDtypeStruct((4608, 768), BF16),
        in_specs=[
            tall,
            pl.BlockSpec((512, 256), lambda i: (0, 0)),
            tall,
            pl.BlockSpec((256, 256), lambda i: (0, 0)),
        ],
        out_specs=pl.BlockSpec((rows, 768), lambda i: (i, 0)),
        compiler_params=params(56),
        cost_estimate=cost(2 * 4608 * 768 * 256, 12000000),
    )(n, proj, g, o)


def sided_products_kernel(flip, count, place_ref, *refs):
    pairs, out_ref = [refs[2 * i : 2 * i + 2] for i in range(count)], refs[-1]
    core, x, yhi = place_ref[2], place_ref[3], place_ref[4]
    side = core if flip == 0 else 1 - core
    for ahead in range(4):
        for over in range(2):
            level = yhi if over == 0 else 1 - yhi
            slot = (level * 4 + (x + ahead) % 4) * 2 + side
            at = 0
            for n_ref, proj_ref in pairs:
                columns = proj_ref.shape[0]
                part = mul(n_ref[slot], proj_ref[...], NT).astype(BF16)
                out_ref[ahead, over, :, at : at + columns] = part
                at += columns


def sided_products(flip, place, pairs):
    columns = sum(proj.shape[0] for _, proj in pairs)
    return pl.pallas_call(
        functools.partial(sided_products_kernel, flip, len(pairs)),
        out_shape=jax.ShapeDtypeStruct((4, 2, 288, columns), BF16),
        in_specs=[SMEM] + [VMEM] * (2 * len(pairs)),
        out_specs=VMEM,
        compiler_params=params(24),
        cost_estimate=cost(2304 * 256 * 2 * columns, 5000000),
    )(place, *[part for n, proj in pairs for part in (n.reshape(16, 288, 256), proj)])


def backward_kernel(routes, inputs, place_ref, qkv_ref, p0_ref, p1_ref, wo_ref, w_ref, *refs):
    blocks = refs[:inputs]
    proj_ref, g_out, dn_out, low_ref, high_ref, g_ref, dn, wo, w, sems, w_sems, out_sems = refs[inputs:]
    copies = place_blocks(routes, place_ref, blocks, [g_ref], sems)
    wo_copy = pltpu.make_async_copy(wo_ref, wo, w_sems.at[0])
    wo_copy.start()
    w_copy = pltpu.make_async_copy(w_ref, w, w_sems.at[1])
    w_copy.start()
    q, k, v = qkv_ref[:256], qkv_ref[256:384], qkv_ref[384:]
    v_rows = v.T
    for copy in copies:
        copy.wait()
    leaving = [pltpu.make_async_copy(g_ref, g_out, out_sems.at[2])]
    leaving[0].start()
    wo_copy.wait()
    d_o = mul(wo[...], g_ref[...].reshape(4608, 256), ROW).astype(BF16)
    d_k, d_v = 0.0, 0.0
    for h in range(2):
        here = slice(h * HD, (h + 1) * HD)
        d_oh = d_o[here]
        p = (p0_ref, p1_ref)[h][...]
        dp = mul(v_rows, d_oh, ROW)
        delta = jnp.sum(p * dp, axis=0, keepdims=True)
        ds = (p * (dp - delta) * (HD**-0.5)).astype(BF16)
        proj_ref[here] = mul(k, ds, ROW).astype(BF16)
        d_k = d_k + mul(q[here], ds, NT)
        d_v = d_v + mul(d_oh, p.astype(BF16), NT)
    proj_ref[256:384] = d_k.astype(BF16)
    proj_ref[384:] = d_v.astype(BF16)
    w_copy.wait()
    proj = proj_ref[...]
    for plane in range(2):
        part = mul(w[plane].reshape(2304, 512), proj, ROW).astype(BF16).reshape(8, 288, 256)
        for depth in range(8):
            dn[(depth + 8 - place_ref[1]) % 8, plane] = part[depth]
        copy = pltpu.make_async_copy(dn.at[:, plane], dn_out.at[:, plane], out_sems.at[plane])
        copy.start()
        leaving.append(copy)
    low_ref[...] = dn[4, :, :144]
    high_ref[...] = dn[4, :, 144:]
    for copy in leaving:
        copy.wait()


def backward(place, saved, routes, w_output, weights):
    qkv, probs, _ = saved
    return pl.pallas_call(
        functools.partial(backward_kernel, routes.routes, len(routes.arrays)),
        out_shape=[
            jax.ShapeDtypeStruct((512, 256), BF16),
            jax.ShapeDtypeStruct((2, 8, 288, 256), BF16),
            jax.ShapeDtypeStruct((8, 2, 288, 256), BF16),
            jax.ShapeDtypeStruct((2, 144, 256), BF16),
            jax.ShapeDtypeStruct((2, 144, 256), BF16),
        ],
        in_specs=[SMEM, VMEM, VMEM, VMEM, ANY, ANY] + [ANY] * len(routes.arrays),
        out_specs=[VMEM, ANY, ANY, VMEM, VMEM],
        scratch_shapes=[
            pltpu.VMEM((2, 8, 288, 256), BF16),
            pltpu.VMEM((8, 2, 288, 256), BF16),
            pltpu.VMEM((256, 4608), BF16),
            pltpu.VMEM((2, 8, 288, 512), BF16),
            pltpu.SemaphoreType.DMA((len(routes.routes),)),
            pltpu.SemaphoreType.DMA((2,)),
            pltpu.SemaphoreType.DMA((3,)),
        ],
        compiler_params=params(56),
        cost_estimate=cost(2 * 4608 * 768 * 256, 15000000),
    )(place, qkv, *probs, w_output, weights.reshape(2, 8, 288, 512), *routes.arrays)


def inputs_kernel(place_ref, order_ref, assign_ref, x_ref, g_ref, gains_ref, out_ref, rows, scales, sems):
    section, shard = place_ref[5], place_ref[6]
    own = order_ref[section]
    following = order_ref[lax.rem(section + 1, 16)]
    which = assign_ref[0, 0], assign_ref[0, 1]
    groups = [pl.ds(pl.multiple_of((number // 8) * 8, 8), 8) for number in which]
    copies = [
        pltpu.make_async_copy(gains_ref.at[groups[0]], scales.at[0], sems.at[0]),
        pltpu.make_async_copy(gains_ref.at[groups[1]], scales.at[1], sems.at[1]),
        pltpu.make_async_copy(x_ref.at[own], rows.at[0], sems.at[2]),
        pltpu.make_async_copy(x_ref.at[following], rows.at[1], sems.at[3]),
        pltpu.make_async_copy(g_ref, out_ref.at[1], sems.at[4]),
    ]
    for copy in copies:
        copy.start()
    for copy in copies:
        copy.wait()
    for number, target in ((0, 0), (1, 2)):
        line = jnp.broadcast_to(scales[number, pl.ds(which[number] % 8, 1)], (8, 4608))
        line = pltpu.roll(line, lax.rem(4608 - shard * 288, 4608), 1)
        column = line[:, :384].T[:288, :1]
        out_ref[target] = (rows[number].astype(F32) * column).astype(BF16)


def scaled_inputs(place, order, assign, x, g, gains):
    return pl.pallas_call(
        inputs_kernel,
        out_shape=jax.ShapeDtypeStruct((3, 288, 256), BF16),
        in_specs=[SMEM, SMEM, SMEM, ANY, ANY, ANY],
        out_specs=VMEM,
        scratch_shapes=[
            pltpu.VMEM((2, 288, 256), BF16),
            pltpu.VMEM((2, 8, 4608), F32),
            pltpu.SemaphoreType.DMA((5,)),
        ],
        compiler_params=params(56),
        cost_estimate=cost(0, 1000000),
    )(place, order, assign, x, g, gains)


class Routes:
    def __init__(self):
        self.arrays, self.routes = [], []

    def add(self, array, pieces):
        at = len(self.arrays)
        self.arrays.append(array)
        for row, piece in enumerate(pieces):
            if piece is not None:
                self.routes.append((at, row) + piece)


def scatter_payload(parts, step, up, down):
    if step == 3:
        up = jnp.concatenate([parts[3][:, :144] + up, parts[3][:, 144:]], axis=1)
        down = jnp.concatenate([parts[5][:, :144], parts[5][:, 144:] + down], axis=1)
        return up, down
    return parts[step] + up, parts[8 - step] + down


def scatter_send(up, down):
    return send(up, "tensor", along_z(1)), send(down, "tensor", along_z(-1))


def scatter_total(parts, up, down):
    return parts[0].astype(F32) + up.astype(F32) + down.astype(F32)


def section_first(keep, came):
    up = send(keep[2, 0] + came[2, 0], "section", along_x(1))
    down = send(keep[2, 1] + came[2, 1], "section", along_x(-1))
    return up, down


def section_second(keep, came, up, down):
    near = keep[1] + came[1]
    up = jnp.stack([near[0] + up, near[1]])
    near = keep[3] + came[3]
    down = jnp.stack([near[0], near[1] + down])
    return send(up, "section", along_x(1)), send(down, "section", along_x(-1))


def section_third(keep, came, up, down):
    total = keep[0].astype(F32) + came[0].astype(F32) + up.astype(F32) + down.astype(F32)
    return total[0], send(total[1].astype(BF16), "section", SWAP_YHI)


def forward(n, weights):
    qkv = mul(weights, n, TN).astype(BF16)
    k, v = qkv[256:384], qkv[384:]
    j = lax.broadcasted_iota(jnp.int32, (256, 256), 0)
    i = lax.broadcasted_iota(jnp.int32, (256, 256), 1)
    causal = j <= i
    probs, outs = [], []
    for h in range(2):
        scores = mul(k, qkv[h * HD : (h + 1) * HD], TN) * (HD**-0.5)
        scores = jnp.where(causal, scores, -1e30)
        top = jnp.max(scores, axis=0, keepdims=True)
        expo = jnp.where(causal, jnp.exp(scores - top), 0.0)
        p = expo / jnp.sum(expo, axis=0, keepdims=True)
        probs.append(p)
        outs.append(mul(v, p.astype(BF16), ROW).astype(BF16))
    return qkv, tuple(probs), jnp.concatenate(outs, axis=0)


def tie(value, *others):
    return lax.optimization_barrier((value,) + others)


def body(x_saved, grad_first, gains, assign, order, w_query, w_key, w_value, w_output):
    s = lax.axis_index("section")
    t = lax.axis_index("tensor")
    z, y = t % 8, t // 8
    place = jnp.stack([y, z, s % 2, (s // 2) % 4, s // 8, s, t]).astype(jnp.int32)
    previous = [(i, (i - 1) % 16) for i in range(16)]

    def share(which, shard):
        return lax.dynamic_slice(gains, (which, shard * 288), (1, 288)).reshape(288, 1)

    full = (2, 8, 288, 256)
    plane = (8, 288, 256)

    own = scaled_inputs(
        place, order, assign, jnp.swapaxes(x_saved[0], 1, 2), grad_first[0].T, gains
    )
    other = send(own[:2], "tensor", SWAP_Y)
    ups, downs, swaps = {0: own}, {0: own}, {}
    for step in (1, 2, 3):
        up, down = ups[step - 1], downs[step - 1]
        if step == 3:
            up, down, swaps[1] = lax.optimization_barrier((up, down, swaps[1]))
        ups[step] = send(up, "tensor", along_z(1))
        downs[step] = send(down, "tensor", along_z(-1))
        swaps[step] = send(jnp.concatenate([downs[step][:2], ups[step][:2]]), "tensor", SWAP_Y)
    up, down, swaps[2] = lax.optimization_barrier((ups[3], downs[3], swaps[2]))
    far = send(up[:, :144], "tensor", along_z(1)), send(down[:, 144:], "tensor", along_z(-1))
    routes, g_routes = Routes(), Routes()

    def first_blocks(block, offset, half):
        routes.add(block, [(0, 0, offset, half), None, (1, None, offset, half)])
        g_routes.add(block, [None, (0, 0, offset, half)])

    first_blocks(own, 0, None)
    routes.add(other, [(0, 1, 0, None)])
    g_routes.add(other, [None, (0, 1, 0, None)])
    for step in (1, 2, 3):
        first_blocks(ups[step], -step, None)
        first_blocks(downs[step], step, None)
        routes.add(swaps[step], [(0, 1, step, None), None, (0, 1, -step, None)])
        g_routes.add(swaps[step], [None, (0, 1, step, None), None, (0, 1, -step, None)])
    for half in (0, 1):
        first_blocks(far[half], 4, half)
    swap = send(jnp.concatenate([far[0][:2], far[1][:2]]), "tensor", SWAP_Y)
    routes.add(swap, [(0, 1, 4, 0), None, (0, 1, 4, 1)])
    g_routes.add(swap, [None, (0, 1, 4, 0), None, (0, 1, 4, 1)])
    n1_full, n2_plane = assemble(routes.arrays, routes.routes, [full, plane], place)
    n1_full = n1_full.reshape(4608, 256)
    n2_other = send(n2_plane, "tensor", SWAP_Y)

    g1_next = send(own[1], "section", previous), send(other[1], "section", previous)
    g1_next = jnp.where(y == 0, g1_next[0], g1_next[1]), jnp.where(y == 0, g1_next[1], g1_next[0])
    which_next = send(assign, "section", previous)[0, 0]

    weights = jnp.concatenate([w_query, w_key, w_value], axis=1)
    saved1 = forward(n1_full, weights)
    proj1, g1_full, dn1, low, high = backward(place, saved1, g_routes, w_output, weights)
    scales = jnp.stack([share(which_next, z + 8 * chain) for chain in (0, 1)])
    came = scatter_send(low, high)
    proj1, came = tie(proj1, came)
    came = scatter_send(*scatter_payload(dn1, 3, *came))
    grads1 = both_products(n1_full, proj1, g1_full.reshape(4608, 256), saved1[2])
    payload, grads1, n2_other, scales, g1_next = tie(
        scatter_payload(dn1, 2, *came), grads1, n2_other, scales, g1_next
    )
    came = scatter_send(*payload)
    grads1 = lax.psum_scatter(grads1, "section", scatter_dimension=0, tiled=True)
    n2_full = jnp.where(
        y == 0, jnp.stack([n2_plane, n2_other]), jnp.stack([n2_other, n2_plane])
    ).reshape(4608, 256)
    saved2 = forward(n2_full, weights)
    payload, saved2 = tie(scatter_payload(dn1, 1, *came), saved2)
    came = scatter_send(*payload)
    part1 = scatter_total(dn1, *came).astype(BF16)
    here = send(part1, ("section", "tensor"), to_previous(0))
    there = send(part1, ("section", "tensor"), to_previous(8))

    g2 = []
    routes = Routes()
    for chain in (0, 1):
        total = here[chain].astype(F32) + there[chain].astype(F32)
        shard = (g1_next[chain].astype(F32) + scales[chain] * total).astype(BF16)
        g2.append(shard)
        found, far = ring(shard[None])
        for offset, block in found.items():
            routes.add(block, [(0, 2 + chain, offset, None)])
        for half in (0, 1):
            routes.add(far[half], [(0, 2 + chain, 4, half)])

    proj2, g2_full, dn2, low, high = backward(place, saved2, routes, w_output, weights)
    step1 = scatter_send(low, high)
    g2_full = g2_full.reshape(4608, 256)

    def pairs(proj):
        return [(n2_full, proj[:384])], [(n2_full, proj[384:]), (g2_full, saved2[2])]

    proj2, step1 = tie(proj2, step1)
    came2 = [send(sided_products(1, place, pair), "section", SWAP_CORE) for pair in pairs(proj2)]
    step2 = scatter_send(*scatter_payload(dn2, 3, *step1))
    proj2, step2 = tie(proj2, step2)
    keeps = [sided_products(0, place, pair) for pair in pairs(proj2)]
    firsts = [section_first(keep, there) for keep, there in zip(keeps, came2)]
    step3 = scatter_send(*scatter_payload(dn2, 2, *step2))
    firsts[0], step3 = tie(firsts[0], step3)
    seconds = [section_second(keeps[0], came2[0], *firsts[0])]
    firsts[1], step3 = tie(firsts[1], step3)
    seconds.append(section_second(keeps[1], came2[1], *firsts[1]))
    payload, grads1 = tie(scatter_payload(dn2, 1, *step3), grads1)
    step_came = scatter_send(*payload)
    lasts = [
        section_third(keep, there, *second) for keep, there, second in zip(keeps, came2, seconds)
    ]

    part2 = scatter_total(dn2, *step_came)
    away = jnp.where(y == 0, part2[1], part2[0]).astype(BF16)
    keep = jnp.where(y == 0, part2[0], part2[1])
    dn2_own = keep + send(away, "tensor", SWAP_Y).astype(F32)
    g2_own = jnp.where(y == 0, g2[0], g2[1])
    dx2 = (g2_own.astype(F32) + share(assign[0, 1], t) * dn2_own).astype(BF16)

    def summed(number, start, stop):
        here, there = (part[:, start:stop].astype(F32) for part in lasts[number])
        return grads1[:, number * 384 + start : number * 384 + stop].astype(F32) + here + there

    return (
        dx2.T[None],
        summed(0, 0, 256),
        summed(0, 256, 384),
        summed(1, 0, 128),
        summed(1, 128, 384).T,
    )


def solution(mesh):
    in_specs = (
        P("section", None, None, "tensor"),
        P("section", None, "tensor"),
        P(),
        P("section", None),
        P(),
        P(None, "tensor"),
        P(None, "tensor"),
        P(None, "tensor"),
        P("tensor", None),
    )
    out_specs = (
        P("section", None, "tensor"),
        P("section", "tensor"),
        P("section", "tensor"),
        P("section", "tensor"),
        P("tensor", "section"),
    )
    return jax.shard_map(body, mesh=mesh, in_specs=in_specs, out_specs=out_specs, check_vma=False)
```

```python
import functools

import jax
import jax.numpy as jnp
from jax import lax
from jax.experimental import pallas as pl
from jax.experimental.pallas import tpu as pltpu
from jax.sharding import PartitionSpec as P

HD = 128
F32 = jnp.float32
BF16 = jnp.bfloat16
ROW = (((1,), (0,)), ((), ()))
NT = (((1,), (1,)), ((), ()))
TN = (((0,), (0,)), ((), ()))


def mul(a, b, dims):
    return lax.dot_general(a, b, dims, preferred_element_type=F32)


def along_z(by):
    return [(t, (t & 8) | ((t + by) & 7)) for t in range(16)]


def along_x(by):
    return [(s, (s & 9) | ((((s >> 1) + by) & 3) << 1)) for s in range(16)]


SWAP_Y = [(t, t ^ 8) for t in range(16)]
SWAP_CORE = [(s, s ^ 1) for s in range(16)]
SWAP_YHI = [(s, s ^ 8) for s in range(16)]


def to_previous(flip):
    pairs = []
    for s in range(16):
        for t in range(16):
            pairs.append((s * 16 + t, ((s - 1) % 16) * 16 + (t ^ flip)))
    return pairs


def send(a, axis, pairs):
    return lax.ppermute(a, axis, pairs)


def ring(payload):
    up, down = payload, payload
    found = {0: payload}
    for step in (1, 2, 3):
        up = send(up, "tensor", along_z(1))
        down = send(down, "tensor", along_z(-1))
        found[-step] = up
        found[step] = down
    far = (
        send(up[:, :144], "tensor", along_z(1)),
        send(down[:, 144:], "tensor", along_z(-1)),
    )
    return found, far


def place_blocks(routes, place_ref, ins, outs, sems):
    copies = []
    for number, (source, row, target, plane, offset, half) in enumerate(routes):
        depth = (place_ref[1] + offset) % 8
        if plane is None:
            dst = outs[target].at[depth]
        else:
            level = (place_ref[0] + plane) % 2 if plane < 2 else plane - 2
            dst = outs[target].at[level, depth]
        if half is not None:
            dst = dst.at[pl.ds(half * 144, 144)]
        copy = pltpu.make_async_copy(ins[source].at[row], dst, sems.at[number])
        copy.start()
        copies.append(copy)
    return copies


def assemble_kernel(routes, inputs, place_ref, *refs):
    for copy in place_blocks(routes, place_ref, refs[:inputs], refs[inputs:-1], refs[-1]):
        copy.wait()


ANY = pl.BlockSpec(memory_space=pl.ANY)
SMEM = pl.BlockSpec(memory_space=pltpu.SMEM)
VMEM = pl.BlockSpec(memory_space=pltpu.VMEM)


def params(mib):
    return pltpu.CompilerParams(vmem_limit_bytes=mib * 2**20)


def cost(flops, moved):
    return pl.CostEstimate(flops=flops, bytes_accessed=moved, transcendentals=0)


def assemble(arrays, routes, out_shapes, place):
    return pl.pallas_call(
        functools.partial(assemble_kernel, routes, len(arrays)),
        out_shape=[jax.ShapeDtypeStruct(shape, BF16) for shape in out_shapes],
        in_specs=[SMEM] + [ANY] * len(arrays),
        out_specs=[VMEM] * len(out_shapes),
        scratch_shapes=[pltpu.SemaphoreType.DMA((len(routes),))],
        compiler_params=params(56),
        cost_estimate=cost(0, 10000000),
    )(place, *arrays)


def both_products_kernel(n_ref, proj_ref, g_ref, o_ref, out_ref):
    out_ref[:, :512] = mul(n_ref[...], proj_ref[...], NT).astype(BF16)
    out_ref[:, 512:] = mul(g_ref[...], o_ref[...], NT).astype(BF16)


def both_products(n, proj, g, o):
    rows = 1152
    tall = pl.BlockSpec((rows, 256), lambda i: (i, 0))
    return pl.pallas_call(
        both_products_kernel,
        grid=(4608 // rows,),
        out_shape=jax.ShapeDtypeStruct((4608, 768), BF16),
        in_specs=[
            tall,
            pl.BlockSpec((512, 256), lambda i: (0, 0)),
            tall,
            pl.BlockSpec((256, 256), lambda i: (0, 0)),
        ],
        out_specs=pl.BlockSpec((rows, 768), lambda i: (i, 0)),
        compiler_params=params(56),
        cost_estimate=cost(2 * 4608 * 768 * 256, 12000000),
    )(n, proj, g, o)


def sided_products_kernel(flip, count, place_ref, *refs):
    pairs, out_ref = [refs[2 * i : 2 * i + 2] for i in range(count)], refs[-1]
    core, x, yhi = place_ref[2], place_ref[3], place_ref[4]
    side = core if flip == 0 else 1 - core
    for ahead in range(4):
        for over in range(2):
            level = yhi if over == 0 else 1 - yhi
            slot = (level * 4 + (x + ahead) % 4) * 2 + side
            at = 0
            for n_ref, proj_ref in pairs:
                columns = proj_ref.shape[0]
                part = mul(n_ref[slot], proj_ref[...], NT).astype(BF16)
                out_ref[ahead, over, :, at : at + columns] = part
                at += columns


def sided_products(flip, place, pairs):
    columns = sum(proj.shape[0] for _, proj in pairs)
    return pl.pallas_call(
        functools.partial(sided_products_kernel, flip, len(pairs)),
        out_shape=jax.ShapeDtypeStruct((4, 2, 288, columns), BF16),
        in_specs=[SMEM] + [VMEM] * (2 * len(pairs)),
        out_specs=VMEM,
        compiler_params=params(24),
        cost_estimate=cost(2304 * 256 * 2 * columns, 5000000),
    )(place, *[part for n, proj in pairs for part in (n.reshape(16, 288, 256), proj)])


def backward_kernel(routes, inputs, place_ref, qkv_ref, p0_ref, p1_ref, wo_ref, w_ref, *refs):
    blocks = refs[:inputs]
    proj_ref, g_out, dn_out, low_ref, high_ref, g_ref, dn, wo, w, sems, w_sems, out_sems = refs[inputs:]
    copies = place_blocks(routes, place_ref, blocks, [g_ref], sems)
    wo_copy = pltpu.make_async_copy(wo_ref, wo, w_sems.at[0])
    wo_copy.start()
    w_copy = pltpu.make_async_copy(w_ref, w, w_sems.at[1])
    w_copy.start()
    q, k, v = qkv_ref[:256], qkv_ref[256:384], qkv_ref[384:]
    v_rows = v.T
    for copy in copies:
        copy.wait()
    leaving = [pltpu.make_async_copy(g_ref, g_out, out_sems.at[2])]
    leaving[0].start()
    wo_copy.wait()
    d_o = mul(wo[...], g_ref[...].reshape(4608, 256), ROW).astype(BF16)
    d_k, d_v = 0.0, 0.0
    for h in range(2):
        here = slice(h * HD, (h + 1) * HD)
        d_oh = d_o[here]
        p = (p0_ref, p1_ref)[h][...]
        dp = mul(v_rows, d_oh, ROW)
        delta = jnp.sum(p * dp, axis=0, keepdims=True)
        ds = (p * (dp - delta) * (HD**-0.5)).astype(BF16)
        proj_ref[here] = mul(k, ds, ROW).astype(BF16)
        d_k = d_k + mul(q[here], ds, NT)
        d_v = d_v + mul(d_oh, p.astype(BF16), NT)
    proj_ref[256:384] = d_k.astype(BF16)
    proj_ref[384:] = d_v.astype(BF16)
    w_copy.wait()
    proj = proj_ref[...]
    for plane in range(2):
        part = mul(w[plane].reshape(2304, 512), proj, ROW).astype(BF16).reshape(8, 288, 256)
        for depth in range(8):
            dn[(depth + 8 - place_ref[1]) % 8, plane] = part[depth]
        copy = pltpu.make_async_copy(dn.at[:, plane], dn_out.at[:, plane], out_sems.at[plane])
        copy.start()
        leaving.append(copy)
    low_ref[...] = dn[4, :, :144]
    high_ref[...] = dn[4, :, 144:]
    for copy in leaving:
        copy.wait()


def backward(place, saved, routes, w_output, weights):
    qkv, probs, _ = saved
    return pl.pallas_call(
        functools.partial(backward_kernel, routes.routes, len(routes.arrays)),
        out_shape=[
            jax.ShapeDtypeStruct((512, 256), BF16),
            jax.ShapeDtypeStruct((2, 8, 288, 256), BF16),
            jax.ShapeDtypeStruct((8, 2, 288, 256), BF16),
            jax.ShapeDtypeStruct((2, 144, 256), BF16),
            jax.ShapeDtypeStruct((2, 144, 256), BF16),
        ],
        in_specs=[SMEM, VMEM, VMEM, VMEM, ANY, ANY] + [ANY] * len(routes.arrays),
        out_specs=[VMEM, ANY, ANY, VMEM, VMEM],
        scratch_shapes=[
            pltpu.VMEM((2, 8, 288, 256), BF16),
            pltpu.VMEM((8, 2, 288, 256), BF16),
            pltpu.VMEM((256, 4608), BF16),
            pltpu.VMEM((2, 8, 288, 512), BF16),
            pltpu.SemaphoreType.DMA((len(routes.routes),)),
            pltpu.SemaphoreType.DMA((2,)),
            pltpu.SemaphoreType.DMA((3,)),
        ],
        compiler_params=params(56),
        cost_estimate=cost(2 * 4608 * 768 * 256, 15000000),
    )(place, qkv, *probs, w_output, weights.reshape(2, 8, 288, 512), *routes.arrays)


def inputs_kernel(place_ref, order_ref, assign_ref, x_ref, g_ref, gains_ref, out_ref, rows, scales, sems):
    section, shard = place_ref[5], place_ref[6]
    own = order_ref[section]
    following = order_ref[lax.rem(section + 1, 16)]
    which = assign_ref[0, 0], assign_ref[0, 1]
    groups = [pl.ds(pl.multiple_of((number // 8) * 8, 8), 8) for number in which]
    copies = [
        pltpu.make_async_copy(gains_ref.at[groups[0]], scales.at[0], sems.at[0]),
        pltpu.make_async_copy(gains_ref.at[groups[1]], scales.at[1], sems.at[1]),
        pltpu.make_async_copy(x_ref.at[own], rows.at[0], sems.at[2]),
        pltpu.make_async_copy(x_ref.at[following], rows.at[1], sems.at[3]),
        pltpu.make_async_copy(g_ref, out_ref.at[1], sems.at[4]),
    ]
    for copy in copies:
        copy.start()
    for copy in copies:
        copy.wait()
    for number, target in ((0, 0), (1, 2)):
        line = jnp.broadcast_to(scales[number, pl.ds(which[number] % 8, 1)], (8, 4608))
        line = pltpu.roll(line, lax.rem(4608 - shard * 288, 4608), 1)
        column = line[:, :384].T[:288, :1]
        out_ref[target] = (rows[number].astype(F32) * column).astype(BF16)


def scaled_inputs(place, order, assign, x, g, gains):
    return pl.pallas_call(
        inputs_kernel,
        out_shape=jax.ShapeDtypeStruct((3, 288, 256), BF16),
        in_specs=[SMEM, SMEM, SMEM, ANY, ANY, ANY],
        out_specs=VMEM,
        scratch_shapes=[
            pltpu.VMEM((2, 288, 256), BF16),
            pltpu.VMEM((2, 8, 4608), F32),
            pltpu.SemaphoreType.DMA((5,)),
        ],
        compiler_params=params(56),
        cost_estimate=cost(0, 1000000),
    )(place, order, assign, x, g, gains)


class Routes:
    def __init__(self):
        self.arrays, self.routes = [], []

    def add(self, array, pieces):
        at = len(self.arrays)
        self.arrays.append(array)
        for row, piece in enumerate(pieces):
            if piece is not None:
                self.routes.append((at, row) + piece)


def scatter_payload(parts, step, up, down):
    if step == 3:
        up = jnp.concatenate([parts[3][:, :144] + up, parts[3][:, 144:]], axis=1)
        down = jnp.concatenate([parts[5][:, :144], parts[5][:, 144:] + down], axis=1)
        return up, down
    return parts[step] + up, parts[8 - step] + down


def scatter_send(up, down):
    return send(up, "tensor", along_z(1)), send(down, "tensor", along_z(-1))


def scatter_total(parts, up, down):
    return parts[0].astype(F32) + up.astype(F32) + down.astype(F32)


def section_first(keep, came):
    up = send(keep[2, 0] + came[2, 0], "section", along_x(1))
    down = send(keep[2, 1] + came[2, 1], "section", along_x(-1))
    return up, down


def section_second(keep, came, up, down):
    near = keep[1] + came[1]
    up = jnp.stack([near[0] + up, near[1]])
    near = keep[3] + came[3]
    down = jnp.stack([near[0], near[1] + down])
    return send(up, "section", along_x(1)), send(down, "section", along_x(-1))


def section_third(keep, came, up, down):
    total = keep[0].astype(F32) + came[0].astype(F32) + up.astype(F32) + down.astype(F32)
    return total[0], send(total[1].astype(BF16), "section", SWAP_YHI)


def forward(n, weights):
    qkv = mul(weights, n, TN).astype(BF16)
    k, v = qkv[256:384], qkv[384:]
    j = lax.broadcasted_iota(jnp.int32, (256, 256), 0)
    i = lax.broadcasted_iota(jnp.int32, (256, 256), 1)
    causal = j <= i
    probs, outs = [], []
    for h in range(2):
        scores = mul(k, qkv[h * HD : (h + 1) * HD], TN) * (HD**-0.5)
        scores = jnp.where(causal, scores, -1e30)
        top = jnp.max(scores, axis=0, keepdims=True)
        expo = jnp.where(causal, jnp.exp(scores - top), 0.0)
        p = expo / jnp.sum(expo, axis=0, keepdims=True)
        probs.append(p)
        outs.append(mul(v, p.astype(BF16), ROW).astype(BF16))
    return qkv, tuple(probs), jnp.concatenate(outs, axis=0)


def tie(value, *others):
    return lax.optimization_barrier((value,) + others)


def body(x_saved, grad_first, gains, assign, order, w_query, w_key, w_value, w_output):
    s = lax.axis_index("section")
    t = lax.axis_index("tensor")
    z, y = t % 8, t // 8
    place = jnp.stack([y, z, s % 2, (s // 2) % 4, s // 8, s, t]).astype(jnp.int32)
    previous = [(i, (i - 1) % 16) for i in range(16)]

    def share(which, shard):
        return lax.dynamic_slice(gains, (which, shard * 288), (1, 288)).reshape(288, 1)

    full = (2, 8, 288, 256)
    plane = (8, 288, 256)

    own = scaled_inputs(
        place, order, assign, jnp.swapaxes(x_saved[0], 1, 2), grad_first[0].T, gains
    )
    other = send(own[:2], "tensor", SWAP_Y)
    ups, downs, swaps = {0: own}, {0: own}, {}
    for step in (1, 2, 3):
        up, down = ups[step - 1], downs[step - 1]
        if step == 3:
            up, down, swaps[1] = lax.optimization_barrier((up, down, swaps[1]))
        ups[step] = send(up, "tensor", along_z(1))
        downs[step] = send(down, "tensor", along_z(-1))
        swaps[step] = send(jnp.concatenate([downs[step][:2], ups[step][:2]]), "tensor", SWAP_Y)
    up, down, swaps[2] = lax.optimization_barrier((ups[3], downs[3], swaps[2]))
    far = send(up[:, :144], "tensor", along_z(1)), send(down[:, 144:], "tensor", along_z(-1))
    routes, g_routes = Routes(), Routes()

    def first_blocks(block, offset, half):
        routes.add(block, [(0, 0, offset, half), None, (1, None, offset, half)])
        g_routes.add(block, [None, (0, 0, offset, half)])

    first_blocks(own, 0, None)
    routes.add(other, [(0, 1, 0, None)])
    g_routes.add(other, [None, (0, 1, 0, None)])
    for step in (1, 2, 3):
        first_blocks(ups[step], -step, None)
        first_blocks(downs[step], step, None)
        routes.add(swaps[step], [(0, 1, step, None), None, (0, 1, -step, None)])
        g_routes.add(swaps[step], [None, (0, 1, step, None), None, (0, 1, -step, None)])
    for half in (0, 1):
        first_blocks(far[half], 4, half)
    swap = send(jnp.concatenate([far[0][:2], far[1][:2]]), "tensor", SWAP_Y)
    routes.add(swap, [(0, 1, 4, 0), None, (0, 1, 4, 1)])
    g_routes.add(swap, [None, (0, 1, 4, 0), None, (0, 1, 4, 1)])
    n1_full, n2_plane = assemble(routes.arrays, routes.routes, [full, plane], place)
    n1_full = n1_full.reshape(4608, 256)
    n2_other = send(n2_plane, "tensor", SWAP_Y)

    g1_next = send(own[1], "section", previous), send(other[1], "section", previous)
    g1_next = jnp.where(y == 0, g1_next[0], g1_next[1]), jnp.where(y == 0, g1_next[1], g1_next[0])
    which_next = send(assign, "section", previous)[0, 0]

    weights = jnp.concatenate([w_query, w_key, w_value], axis=1)
    saved1 = forward(n1_full, weights)
    proj1, g1_full, dn1, low, high = backward(place, saved1, g_routes, w_output, weights)
    scales = jnp.stack([share(which_next, z + 8 * chain) for chain in (0, 1)])
    came = scatter_send(low, high)
    proj1, came = tie(proj1, came)
    came = scatter_send(*scatter_payload(dn1, 3, *came))
    grads1 = both_products(n1_full, proj1, g1_full.reshape(4608, 256), saved1[2])
    payload, grads1, n2_other, scales, g1_next = tie(
        scatter_payload(dn1, 2, *came), grads1, n2_other, scales, g1_next
    )
    came = scatter_send(*payload)
    grads1 = lax.psum_scatter(grads1, "section", scatter_dimension=0, tiled=True)
    n2_full = jnp.where(
        y == 0, jnp.stack([n2_plane, n2_other]), jnp.stack([n2_other, n2_plane])
    ).reshape(4608, 256)
    saved2 = forward(n2_full, weights)
    payload, saved2 = tie(scatter_payload(dn1, 1, *came), saved2)
    came = scatter_send(*payload)
    part1 = scatter_total(dn1, *came).astype(BF16)
    here = send(part1, ("section", "tensor"), to_previous(0))
    there = send(part1, ("section", "tensor"), to_previous(8))

    g2 = []
    routes = Routes()
    for chain in (0, 1):
        total = here[chain].astype(F32) + there[chain].astype(F32)
        shard = (g1_next[chain].astype(F32) + scales[chain] * total).astype(BF16)
        g2.append(shard)
        found, far = ring(shard[None])
        for offset, block in found.items():
            routes.add(block, [(0, 2 + chain, offset, None)])
        for half in (0, 1):
            routes.add(far[half], [(0, 2 + chain, 4, half)])

    proj2, g2_full, dn2, low, high = backward(place, saved2, routes, w_output, weights)
    g2_full = g2_full.reshape(4608, 256)
    pairs = [(n2_full, proj2[:384])], [(n2_full, proj2[384:]), (g2_full, saved2[2])]
    step1 = scatter_send(low, high)
    came2 = [send(sided_products(1, place, pair), "section", SWAP_CORE) for pair in pairs]
    keeps = [sided_products(0, place, pair) for pair in pairs]
    step1, came2, keeps = tie(step1, came2, keeps)
    step2 = scatter_send(*scatter_payload(dn2, 3, *step1))
    firsts = [section_first(keep, there) for keep, there in zip(keeps, came2)]
    step2, firsts = tie(step2, firsts)
    step3 = scatter_send(*scatter_payload(dn2, 2, *step2))
    second0 = section_second(keeps[0], came2[0], *firsts[0])
    step3, second0, grads1 = tie(step3, second0, grads1)
    step_came = scatter_send(*scatter_payload(dn2, 1, *step3))
    second1 = section_second(keeps[1], came2[1], *firsts[1])
    last0 = section_third(keeps[0], came2[0], *second0)
    step_came, second1, last0 = tie(step_came, second1, last0)
    lasts = [last0, section_third(keeps[1], came2[1], *second1)]

    part2 = scatter_total(dn2, *step_came)
    away = jnp.where(y == 0, part2[1], part2[0]).astype(BF16)
    keep = jnp.where(y == 0, part2[0], part2[1])
    dn2_own = keep + send(away, "tensor", SWAP_Y).astype(F32)
    g2_own = jnp.where(y == 0, g2[0], g2[1])
    dx2 = (g2_own.astype(F32) + share(assign[0, 1], t) * dn2_own).astype(BF16)

    def summed(number, start, stop):
        here, there = (part[:, start:stop].astype(F32) for part in lasts[number])
        return grads1[:, number * 384 + start : number * 384 + stop].astype(F32) + here + there

    return (
        dx2.T[None],
        summed(0, 0, 256),
        summed(0, 256, 384),
        summed(1, 0, 128),
        summed(1, 128, 384).T,
    )


def solution(mesh):
    in_specs = (
        P("section", None, None, "tensor"),
        P("section", None, "tensor"),
        P(),
        P("section", None),
        P(),
        P(None, "tensor"),
        P(None, "tensor"),
        P(None, "tensor"),
        P("tensor", None),
    )
    out_specs = (
        P("section", None, "tensor"),
        P("section", "tensor"),
        P("section", "tensor"),
        P("section", "tensor"),
        P("tensor", "section"),
    )
    return jax.shard_map(body, mesh=mesh, in_specs=in_specs, out_specs=out_specs, check_vma=False)
```

```python
import functools

import jax
import jax.numpy as jnp
from jax import lax
from jax.experimental import pallas as pl
from jax.experimental.pallas import tpu as pltpu
from jax.sharding import PartitionSpec as P

HD = 128
F32 = jnp.float32
BF16 = jnp.bfloat16
ROW = (((1,), (0,)), ((), ()))
NT = (((1,), (1,)), ((), ()))
TN = (((0,), (0,)), ((), ()))


def mul(a, b, dims):
    return lax.dot_general(a, b, dims, preferred_element_type=F32)


def along_z(by):
    return [(t, (t & 8) | ((t + by) & 7)) for t in range(16)]


def along_x(by):
    return [(s, (s & 9) | ((((s >> 1) + by) & 3) << 1)) for s in range(16)]


SWAP_Y = [(t, t ^ 8) for t in range(16)]
SWAP_CORE = [(s, s ^ 1) for s in range(16)]
SWAP_YHI = [(s, s ^ 8) for s in range(16)]


def to_previous(flip):
    pairs = []
    for s in range(16):
        for t in range(16):
            pairs.append((s * 16 + t, ((s - 1) % 16) * 16 + (t ^ flip)))
    return pairs


def send(a, axis, pairs):
    return lax.ppermute(a, axis, pairs)


def ring(payload):
    up, down = payload, payload
    found = {0: payload}
    for step in (1, 2, 3):
        up = send(up, "tensor", along_z(1))
        down = send(down, "tensor", along_z(-1))
        found[-step] = up
        found[step] = down
    far = (
        send(up[:, :144], "tensor", along_z(1)),
        send(down[:, 144:], "tensor", along_z(-1)),
    )
    return found, far


def place_blocks(routes, place_ref, ins, outs, sems):
    copies = []
    for number, (source, row, target, plane, offset, half) in enumerate(routes):
        depth = (place_ref[1] + offset) % 8
        if plane is None:
            dst = outs[target].at[depth]
        else:
            level = (place_ref[0] + plane) % 2 if plane < 2 else plane - 2
            dst = outs[target].at[level, depth]
        if half is not None:
            dst = dst.at[pl.ds(half * 144, 144)]
        copy = pltpu.make_async_copy(ins[source].at[row], dst, sems.at[number])
        copy.start()
        copies.append(copy)
    return copies


def assemble_kernel(routes, inputs, place_ref, *refs):
    for copy in place_blocks(routes, place_ref, refs[:inputs], refs[inputs:-1], refs[-1]):
        copy.wait()


ANY = pl.BlockSpec(memory_space=pl.ANY)
SMEM = pl.BlockSpec(memory_space=pltpu.SMEM)
VMEM = pl.BlockSpec(memory_space=pltpu.VMEM)


def params(mib):
    return pltpu.CompilerParams(vmem_limit_bytes=mib * 2**20)


def cost(flops, moved):
    return pl.CostEstimate(flops=flops, bytes_accessed=moved, transcendentals=0)


def assemble(arrays, routes, out_shapes, place):
    return pl.pallas_call(
        functools.partial(assemble_kernel, routes, len(arrays)),
        out_shape=[jax.ShapeDtypeStruct(shape, BF16) for shape in out_shapes],
        in_specs=[SMEM] + [ANY] * len(arrays),
        out_specs=[VMEM] * len(out_shapes),
        scratch_shapes=[pltpu.SemaphoreType.DMA((len(routes),))],
        compiler_params=params(56),
        cost_estimate=cost(0, 10000000),
    )(place, *arrays)


def both_products_kernel(n_ref, proj_ref, g_ref, o_ref, out_ref):
    out_ref[:, :512] = mul(n_ref[...], proj_ref[...], NT).astype(BF16)
    out_ref[:, 512:] = mul(g_ref[...], o_ref[...], NT).astype(BF16)


def both_products(n, proj, g, o):
    rows = 1152
    tall = pl.BlockSpec((rows, 256), lambda i: (i, 0))
    return pl.pallas_call(
        both_products_kernel,
        grid=(4608 // rows,),
        out_shape=jax.ShapeDtypeStruct((4608, 768), BF16),
        in_specs=[
            tall,
            pl.BlockSpec((512, 256), lambda i: (0, 0)),
            tall,
            pl.BlockSpec((256, 256), lambda i: (0, 0)),
        ],
        out_specs=pl.BlockSpec((rows, 768), lambda i: (i, 0)),
        compiler_params=params(56),
        cost_estimate=cost(2 * 4608 * 768 * 256, 12000000),
    )(n, proj, g, o)


def sided_products_kernel(flip, count, place_ref, *refs):
    pairs, out_ref = [refs[2 * i : 2 * i + 2] for i in range(count)], refs[-1]
    core, x, yhi = place_ref[2], place_ref[3], place_ref[4]
    side = core if flip == 0 else 1 - core
    for ahead in range(4):
        for over in range(2):
            level = yhi if over == 0 else 1 - yhi
            slot = (level * 4 + (x + ahead) % 4) * 2 + side
            at = 0
            for n_ref, proj_ref in pairs:
                columns = proj_ref.shape[0]
                part = mul(n_ref[slot], proj_ref[...], NT).astype(BF16)
                out_ref[ahead, over, :, at : at + columns] = part
                at += columns


def sided_products(flip, place, pairs):
    columns = sum(proj.shape[0] for _, proj in pairs)
    return pl.pallas_call(
        functools.partial(sided_products_kernel, flip, len(pairs)),
        out_shape=jax.ShapeDtypeStruct((4, 2, 288, columns), BF16),
        in_specs=[SMEM] + [VMEM] * (2 * len(pairs)),
        out_specs=VMEM,
        compiler_params=params(24),
        cost_estimate=cost(2304 * 256 * 2 * columns, 5000000),
    )(place, *[part for n, proj in pairs for part in (n.reshape(16, 288, 256), proj)])


def backward_kernel(routes, inputs, place_ref, qkv_ref, p0_ref, p1_ref, wo_ref, w_ref, *refs):
    blocks = refs[:inputs]
    proj_ref, g_out, dn_out, low_ref, high_ref, g_ref, dn, wo, w, sems, w_sems, out_sems = refs[inputs:]
    copies = place_blocks(routes, place_ref, blocks, [g_ref], sems)
    wo_copy = pltpu.make_async_copy(wo_ref, wo, w_sems.at[0])
    wo_copy.start()
    w_copy = pltpu.make_async_copy(w_ref, w, w_sems.at[1])
    w_copy.start()
    q, k, v = qkv_ref[:256], qkv_ref[256:384], qkv_ref[384:]
    v_rows = v.T
    for copy in copies:
        copy.wait()
    leaving = [pltpu.make_async_copy(g_ref, g_out, out_sems.at[2])]
    leaving[0].start()
    wo_copy.wait()
    d_o = mul(wo[...], g_ref[...].reshape(4608, 256), ROW).astype(BF16)
    d_k, d_v = 0.0, 0.0
    for h in range(2):
        here = slice(h * HD, (h + 1) * HD)
        d_oh = d_o[here]
        p = (p0_ref, p1_ref)[h][...]
        dp = mul(v_rows, d_oh, ROW)
        delta = jnp.sum(p * dp, axis=0, keepdims=True)
        ds = (p * (dp - delta) * (HD**-0.5)).astype(BF16)
        proj_ref[here] = mul(k, ds, ROW).astype(BF16)
        d_k = d_k + mul(q[here], ds, NT)
        d_v = d_v + mul(d_oh, p.astype(BF16), NT)
    proj_ref[256:384] = d_k.astype(BF16)
    proj_ref[384:] = d_v.astype(BF16)
    w_copy.wait()
    proj = proj_ref[...]
    for plane in range(2):
        part = mul(w[plane].reshape(2304, 512), proj, ROW).astype(BF16).reshape(8, 288, 256)
        for depth in range(8):
            dn[(depth + 8 - place_ref[1]) % 8, plane] = part[depth]
        copy = pltpu.make_async_copy(dn.at[:, plane], dn_out.at[:, plane], out_sems.at[plane])
        copy.start()
        leaving.append(copy)
    low_ref[...] = dn[4, :, :144]
    high_ref[...] = dn[4, :, 144:]
    for copy in leaving:
        copy.wait()


def backward(place, saved, routes, w_output, weights):
    qkv, probs, _ = saved
    return pl.pallas_call(
        functools.partial(backward_kernel, routes.routes, len(routes.arrays)),
        out_shape=[
            jax.ShapeDtypeStruct((512, 256), BF16),
            jax.ShapeDtypeStruct((2, 8, 288, 256), BF16),
            jax.ShapeDtypeStruct((8, 2, 288, 256), BF16),
            jax.ShapeDtypeStruct((2, 144, 256), BF16),
            jax.ShapeDtypeStruct((2, 144, 256), BF16),
        ],
        in_specs=[SMEM, VMEM, VMEM, VMEM, ANY, ANY] + [ANY] * len(routes.arrays),
        out_specs=[VMEM, ANY, ANY, VMEM, VMEM],
        scratch_shapes=[
            pltpu.VMEM((2, 8, 288, 256), BF16),
            pltpu.VMEM((8, 2, 288, 256), BF16),
            pltpu.VMEM((256, 4608), BF16),
            pltpu.VMEM((2, 8, 288, 512), BF16),
            pltpu.SemaphoreType.DMA((len(routes.routes),)),
            pltpu.SemaphoreType.DMA((2,)),
            pltpu.SemaphoreType.DMA((3,)),
        ],
        compiler_params=params(56),
        cost_estimate=cost(2 * 4608 * 768 * 256, 15000000),
    )(place, qkv, *probs, w_output, weights.reshape(2, 8, 288, 512), *routes.arrays)


def inputs_kernel(place_ref, order_ref, assign_ref, x_ref, g_ref, gains_ref, out_ref, rows, scales, sems):
    section, shard = place_ref[5], place_ref[6]
    own = order_ref[section]
    following = order_ref[lax.rem(section + 1, 16)]
    which = assign_ref[0, 0], assign_ref[0, 1]
    groups = [pl.ds(pl.multiple_of((number // 8) * 8, 8), 8) for number in which]
    copies = [
        pltpu.make_async_copy(gains_ref.at[groups[0]], scales.at[0], sems.at[0]),
        pltpu.make_async_copy(gains_ref.at[groups[1]], scales.at[1], sems.at[1]),
        pltpu.make_async_copy(x_ref.at[own], rows.at[0], sems.at[2]),
        pltpu.make_async_copy(x_ref.at[following], rows.at[1], sems.at[3]),
        pltpu.make_async_copy(g_ref, out_ref.at[1], sems.at[4]),
    ]
    for copy in copies:
        copy.start()
    for copy in copies:
        copy.wait()
    for number, target in ((0, 0), (1, 2)):
        line = jnp.broadcast_to(scales[number, pl.ds(which[number] % 8, 1)], (8, 4608))
        line = pltpu.roll(line, lax.rem(4608 - shard * 288, 4608), 1)
        column = line[:, :384].T[:288, :1]
        out_ref[target] = (rows[number].astype(F32) * column).astype(BF16)


def scaled_inputs(place, order, assign, x, g, gains):
    return pl.pallas_call(
        inputs_kernel,
        out_shape=jax.ShapeDtypeStruct((3, 288, 256), BF16),
        in_specs=[SMEM, SMEM, SMEM, ANY, ANY, ANY],
        out_specs=VMEM,
        scratch_shapes=[
            pltpu.VMEM((2, 288, 256), BF16),
            pltpu.VMEM((2, 8, 4608), F32),
            pltpu.SemaphoreType.DMA((5,)),
        ],
        compiler_params=params(56),
        cost_estimate=cost(0, 1000000),
    )(place, order, assign, x, g, gains)


class Routes:
    def __init__(self):
        self.arrays, self.routes = [], []

    def add(self, array, pieces):
        at = len(self.arrays)
        self.arrays.append(array)
        for row, piece in enumerate(pieces):
            if piece is not None:
                self.routes.append((at, row) + piece)


def scatter_payload(parts, step, up, down):
    if step == 3:
        up = jnp.concatenate([parts[3][:, :144] + up, parts[3][:, 144:]], axis=1)
        down = jnp.concatenate([parts[5][:, :144], parts[5][:, 144:] + down], axis=1)
        return up, down
    return parts[step] + up, parts[8 - step] + down


def scatter_send(up, down):
    return send(up, "tensor", along_z(1)), send(down, "tensor", along_z(-1))


def scatter_total(parts, up, down):
    return parts[0].astype(F32) + up.astype(F32) + down.astype(F32)


def section_first(keep, came):
    up = send(keep[2, 0] + came[2, 0], "section", along_x(1))
    down = send(keep[2, 1] + came[2, 1], "section", along_x(-1))
    return up, down


def section_second(keep, came, up, down):
    near = keep[1] + came[1]
    up = jnp.stack([near[0] + up, near[1]])
    near = keep[3] + came[3]
    down = jnp.stack([near[0], near[1] + down])
    return send(up, "section", along_x(1)), send(down, "section", along_x(-1))


def section_third(keep, came, up, down):
    total = keep[0].astype(F32) + came[0].astype(F32) + up.astype(F32) + down.astype(F32)
    return total[0], send(total[1].astype(BF16), "section", SWAP_YHI)


def forward(n, weights):
    qkv = mul(weights, n, TN).astype(BF16)
    k, v = qkv[256:384], qkv[384:]
    j = lax.broadcasted_iota(jnp.int32, (256, 256), 0)
    i = lax.broadcasted_iota(jnp.int32, (256, 256), 1)
    causal = j <= i
    probs, outs = [], []
    for h in range(2):
        scores = mul(k, qkv[h * HD : (h + 1) * HD], TN) * (HD**-0.5)
        scores = jnp.where(causal, scores, -1e30)
        top = jnp.max(scores, axis=0, keepdims=True)
        expo = jnp.where(causal, jnp.exp(scores - top), 0.0)
        p = expo / jnp.sum(expo, axis=0, keepdims=True)
        probs.append(p)
        outs.append(mul(v, p.astype(BF16), ROW).astype(BF16))
    return qkv, tuple(probs), jnp.concatenate(outs, axis=0)


def tie(value, *others):
    return lax.optimization_barrier((value,) + others)


def body(x_saved, grad_first, gains, assign, order, w_query, w_key, w_value, w_output):
    s = lax.axis_index("section")
    t = lax.axis_index("tensor")
    z, y = t % 8, t // 8
    place = jnp.stack([y, z, s % 2, (s // 2) % 4, s // 8, s, t]).astype(jnp.int32)
    previous = [(i, (i - 1) % 16) for i in range(16)]

    def share(which, shard):
        return lax.dynamic_slice(gains, (which, shard * 288), (1, 288)).reshape(288, 1)

    full = (2, 8, 288, 256)
    plane = (8, 288, 256)

    own = scaled_inputs(
        place, order, assign, jnp.swapaxes(x_saved[0], 1, 2), grad_first[0].T, gains
    )
    other = send(own[:2], "tensor", SWAP_Y)
    ups, downs, swaps = {0: own}, {0: own}, {}
    for step in (1, 2, 3):
        up, down = ups[step - 1], downs[step - 1]
        if step == 3:
            up, down, swaps[1] = lax.optimization_barrier((up, down, swaps[1]))
        ups[step] = send(up, "tensor", along_z(1))
        downs[step] = send(down, "tensor", along_z(-1))
        swaps[step] = send(jnp.stack([downs[step][1], ups[step][1]]), "tensor", SWAP_Y)
    up, down, swaps[2] = lax.optimization_barrier((ups[3], downs[3], swaps[2]))
    far = send(up[:, :144], "tensor", along_z(1)), send(down[:, 144:], "tensor", along_z(-1))
    found_n, far_n = ring(other[:1])
    routes, g_routes = Routes(), Routes()

    def first_blocks(block, offset, half):
        routes.add(block, [(0, 0, offset, half), None, (1, None, offset, half)])
        g_routes.add(block, [None, (0, 0, offset, half)])

    first_blocks(own, 0, None)
    for step in (1, 2, 3):
        first_blocks(ups[step], -step, None)
        first_blocks(downs[step], step, None)
        g_routes.add(swaps[step], [(0, 1, step, None), (0, 1, -step, None)])
    for half in (0, 1):
        first_blocks(far[half], 4, half)
        routes.add(far_n[half], [(0, 1, 4, half)])
    swap = send(jnp.stack([far[0][1], far[1][1]]), "tensor", SWAP_Y)
    for offset, block in found_n.items():
        if offset:
            routes.add(block, [(0, 1, offset, None)])
    routes.add(other, [(0, 1, 0, None)])
    g_routes.add(other, [None, (0, 1, 0, None)])
    n1_full, n2_plane = assemble(routes.arrays, routes.routes, [full, plane], place)
    n1_full, swap = lax.optimization_barrier((n1_full.reshape(4608, 256), swap))
    g_routes.add(swap, [(0, 1, 4, 0), (0, 1, 4, 1)])
    n2_other = send(n2_plane, "tensor", SWAP_Y)

    g1_next = send(own[1], "section", previous), send(other[1], "section", previous)
    g1_next = jnp.where(y == 0, g1_next[0], g1_next[1]), jnp.where(y == 0, g1_next[1], g1_next[0])
    which_next = send(assign, "section", previous)[0, 0]

    weights = jnp.concatenate([w_query, w_key, w_value], axis=1)
    saved1 = forward(n1_full, weights)
    proj1, g1_full, dn1, low, high = backward(place, saved1, g_routes, w_output, weights)
    scales = jnp.stack([share(which_next, z + 8 * chain) for chain in (0, 1)])
    came = scatter_send(low, high)
    proj1, came = tie(proj1, came)
    came = scatter_send(*scatter_payload(dn1, 3, *came))
    grads1 = both_products(n1_full, proj1, g1_full.reshape(4608, 256), saved1[2])
    payload, grads1, n2_other, scales, g1_next = tie(
        scatter_payload(dn1, 2, *came), grads1, n2_other, scales, g1_next
    )
    came = scatter_send(*payload)
    grads1 = lax.psum_scatter(grads1, "section", scatter_dimension=0, tiled=True)
    n2_full = jnp.where(
        y == 0, jnp.stack([n2_plane, n2_other]), jnp.stack([n2_other, n2_plane])
    ).reshape(4608, 256)
    saved2 = forward(n2_full, weights)
    payload, saved2 = tie(scatter_payload(dn1, 1, *came), saved2)
    came = scatter_send(*payload)
    part1 = scatter_total(dn1, *came).astype(BF16)
    here = send(part1, ("section", "tensor"), to_previous(0))
    there = send(part1, ("section", "tensor"), to_previous(8))

    g2 = []
    routes = Routes()
    for chain in (0, 1):
        total = here[chain].astype(F32) + there[chain].astype(F32)
        shard = (g1_next[chain].astype(F32) + scales[chain] * total).astype(BF16)
        g2.append(shard)
        found, far = ring(shard[None])
        for offset, block in found.items():
            routes.add(block, [(0, 2 + chain, offset, None)])
        for half in (0, 1):
            routes.add(far[half], [(0, 2 + chain, 4, half)])

    proj2, g2_full, dn2, low, high = backward(place, saved2, routes, w_output, weights)
    step_came = scatter_send(low, high)

    g2_full = g2_full.reshape(4608, 256)

    def pairs(proj):
        return [(n2_full, proj[:384])], [(n2_full, proj[384:]), (g2_full, saved2[2])]

    came2 = [send(sided_products(1, place, pair), "section", SWAP_CORE) for pair in pairs(proj2)]
    proj2, step_came = tie(proj2, step_came)
    keeps = [sided_products(0, place, pair) for pair in pairs(proj2)]
    step2 = scatter_send(*scatter_payload(dn2, 3, *step_came))
    first0 = section_first(keeps[0], came2[0])
    came2[1], step2 = tie(came2[1], step2)
    first1 = section_first(keeps[1], came2[1])
    payload, first0, grads1 = tie(scatter_payload(dn2, 2, *step2), first0, grads1)
    step3 = scatter_send(*payload)
    second0 = section_second(keeps[0], came2[0], *first0)
    payload, first1 = tie(scatter_payload(dn2, 1, *step3), first1)
    step_came = scatter_send(*payload)
    first1, step3 = tie(first1, step3)
    second1 = section_second(keeps[1], came2[1], *first1)
    lasts = [
        section_third(keep, there, *second)
        for keep, there, second in zip(keeps, came2, (second0, second1))
    ]

    part2 = scatter_total(dn2, *step_came)
    away = jnp.where(y == 0, part2[1], part2[0]).astype(BF16)
    keep = jnp.where(y == 0, part2[0], part2[1])
    dn2_own = keep + send(away, "tensor", SWAP_Y).astype(F32)
    g2_own = jnp.where(y == 0, g2[0], g2[1])
    dx2 = (g2_own.astype(F32) + share(assign[0, 1], t) * dn2_own).astype(BF16)

    def summed(number, start, stop):
        here, there = (part[:, start:stop].astype(F32) for part in lasts[number])
        return grads1[:, number * 384 + start : number * 384 + stop].astype(F32) + here + there

    return (
        dx2.T[None],
        summed(0, 0, 256),
        summed(0, 256, 384),
        summed(1, 0, 128),
        summed(1, 128, 384).T,
    )


def solution(mesh):
    in_specs = (
        P("section", None, None, "tensor"),
        P("section", None, "tensor"),
        P(),
        P("section", None),
        P(),
        P(None, "tensor"),
        P(None, "tensor"),
        P(None, "tensor"),
        P("tensor", None),
    )
    out_specs = (
        P("section", None, "tensor"),
        P("section", "tensor"),
        P("section", "tensor"),
        P("section", "tensor"),
        P("tensor", "section"),
    )
    return jax.shard_map(body, mesh=mesh, in_specs=in_specs, out_specs=out_specs, check_vma=False)
```
